128 devices in a mesh: grp: 8 (over y, x_lo), sub: 16 (over x_hi, z, core).
Axes of the slice: x: 4 (x_hi: 2, x_lo: 2; x = x_hi * 2 + x_lo), y: 4, z: 4, core: 2. Of those that a mesh axis runs over, the one named last changes fastest.
Arguments:
- records: bfloat16 [4096, 2, 2048], P(('grp', 'sub')), may hold values from -6 to 6
- ref_bin: int32 [8, 512, 16, 256], P('grp', None, 'sub'), may hold values from 0 to 63
- ref_table: bfloat16 [64, 8], replicated
Outputs:
- adjoint: float32 [4096, 2, 2048], P(('grp', 'sub'))
The draws below stay inside these ranges and needn't reach their ends.
All inputs are finite; a program needn't handle non-finite values.
Results may differ from the reference program's by a relative error of at most 0.007.
Values may be sent and summed in bfloat16 or wider, within the bound.
A program may use at most 128 MiB of HBM per device.

```python
import math
import jax
import jax.numpy as jnp
from jax import lax

STAT_DEV = 32
FREQS = 2048
BANDS = 4
DIST_BINS = 64
BAND_WIDTH = 512
STATIONS = 4096
N_GRP = 8
N_SUB = 16


def draw_ref_bin(key, part):
    key = jax.random.fold_in(key, 3)
    heavy_count = DIST_BINS // 4
    key_pick, key_heavy, key_drawn = jax.random.split(key, 3)
    block_shape = (N_GRP, N_SUB, 1, N_SUB, N_GRP, 1)
    picked = jax.random.randint(key_pick, block_shape, 0, 16)
    picked = picked.at[0, 0, 0, 0, 0, 0].set(0)
    heavy_bin = DIST_BINS - 1 - jax.random.randint(key_heavy, block_shape, 0, heavy_count)
    heavy_bin = heavy_bin.at[0, 0, 0, 0, 0, 0].set(DIST_BINS - 1)
    full_shape = (N_GRP, N_SUB, STAT_DEV, N_SUB, N_GRP, STAT_DEV)
    drawn = jax.random.randint(key_drawn, full_shape, 0, DIST_BINS - heavy_count)
    chosen = jnp.where(picked == 0, jnp.broadcast_to(heavy_bin, full_shape), drawn)
    return chosen.reshape(N_GRP, N_SUB * STAT_DEV, N_SUB, N_GRP * STAT_DEV).astype(jnp.int32)


def draw_ref_table(key, part):
    key = jax.random.fold_in(key, 5)
    heavy_count = DIST_BINS // 4
    index = jnp.arange(DIST_BINS)[:, None]
    scales = jnp.where(index >= DIST_BINS - heavy_count, 8.0, 1.5)
    values = jnp.clip(jax.random.normal(key, (DIST_BINS, 2 * BANDS), jnp.float32), -3.0, 3.0)
    return (values * scales).astype(jnp.bfloat16)


def levels(rng, shape, cuts, low, largest):
    level, own = 1.0, jax.random.fold_in(rng, 6)
    for dim, parts in cuts:
        draws = jnp.exp(jax.random.uniform(jax.random.fold_in(own, dim), (parts,), jnp.float32, low / len(cuts), largest / len(cuts)))
        level = level * jnp.repeat(draws, shape[dim] // parts).reshape([-1 if axis == dim else 1 for axis in range(len(shape))])
    return level


def bell_draw(key, dims, spread, limit, cuts=(), held_as=jnp.bfloat16):
    result = jax.random.normal(key, dims, jnp.float32) * spread
    if len(cuts) > 0:
        result = levels(key, dims, cuts, -0.22, 0.18) * result
    return jnp.clip(result, min=-limit, max=limit).astype(held_as)


def setup_inputs(seed: int = 0) -> dict:
    splits = jax.random.split(jax.random.key(seed), 4)
    return {
        "records": bell_draw(splits[0], (STATIONS, 2, FREQS), 1.0, 6.0, ((0, 128),)),
        "ref_bin": draw_ref_bin(jax.random.fold_in(splits[3], 71), 0),
        "ref_table": draw_ref_table(jax.random.fold_in(splits[3], 71), 0),
    }


def pair_tile(rows, cols, bins, table):
    row_count = rows.shape[0]
    col_count = cols.shape[0]
    scale = 1.0 / math.sqrt(BAND_WIDTH)
    row_real = rows[:, 0].astype(jnp.float32).reshape(row_count, BANDS, BAND_WIDTH)
    row_imag = rows[:, 1].astype(jnp.float32).reshape(row_count, BANDS, BAND_WIDTH)
    column_real_part = cols[:, 0].astype(jnp.float32).reshape(col_count, BANDS, BAND_WIDTH)
    column_imaginary = cols[:, 1].astype(jnp.float32).reshape(col_count, BANDS, BAND_WIDTH)

    def cross(left, right):
        return jnp.einsum('rbf,kbf->rbk', left, right)
    corr_real = (cross(row_real, column_real_part) + cross(row_imag, column_imaginary)) * scale
    corr_imag = (cross(row_imag, column_real_part) - cross(row_real, column_imaginary)) * scale
    looked = table.astype(jnp.float32)[bins]
    ref_real = jnp.transpose(looked[:, :, :BANDS], (0, 2, 1))
    ref_imag = jnp.transpose(looked[:, :, BANDS:], (0, 2, 1))
    residual_real_part = lax.optimization_barrier((corr_real - ref_real).astype(jnp.bfloat16)).astype(jnp.float32)
    residual_imaginary = lax.optimization_barrier((corr_imag - ref_imag).astype(jnp.bfloat16)).astype(jnp.float32)

    def toward_columns(left, right):
        return jnp.einsum('rbk,kbf->rbf', left, right)

    def to_rows(left, right):
        return jnp.einsum('rbk,rbf->kbf', left, right)
    row_re = toward_columns(residual_real_part, column_real_part) - toward_columns(residual_imaginary, column_imaginary)
    row_im = toward_columns(residual_real_part, column_imaginary) + toward_columns(residual_imaginary, column_real_part)
    col_re = to_rows(residual_real_part, row_real) + to_rows(residual_imaginary, row_imag)
    col_im = to_rows(residual_real_part, row_imag) - to_rows(residual_imaginary, row_real)
    row_term = jnp.stack((row_re, row_im), axis=1).reshape(row_count, 2, FREQS)
    col_term = jnp.stack((col_re, col_im), axis=1).reshape(col_count, 2, FREQS)
    return (row_term, col_term)

def reference(records, ref_bin, ref_table):
    by_device = records.reshape(N_GRP, N_SUB, STAT_DEV, 2, FREQS)

    def group_step(col_total, group):
        rows = by_device[group].reshape(N_SUB * STAT_DEV, 2, FREQS)

        def block_step(row_total, block):
            cols = by_device[:, block].reshape(N_GRP * STAT_DEV, 2, FREQS)
            bins = ref_bin[group, :, block, :]
            row_term, col_term = pair_tile(rows, cols, bins, ref_table)
            return (row_total + row_term, col_term)
        start_rows = jnp.zeros((N_SUB * STAT_DEV, 2, FREQS), jnp.float32)
        row_total, col_terms = lax.scan(block_step, start_rows, jnp.arange(N_SUB, dtype=jnp.int32))
        return (col_total + col_terms, row_total)
    start_cols = jnp.zeros((N_SUB, N_GRP * STAT_DEV, 2, FREQS), jnp.float32)
    col_total, row_totals = lax.scan(group_step, start_cols, jnp.arange(N_GRP, dtype=jnp.int32))
    row_part = row_totals.reshape(STATIONS, 2, FREQS)
    col_part = jnp.transpose(col_total.reshape(N_SUB, N_GRP, STAT_DEV, 2, FREQS), (1, 0, 2, 3, 4)).reshape(STATIONS, 2, FREQS)
    return (row_part + col_part) / math.sqrt(STATIONS)
```

```python
import math

import jax
import jax.numpy as jnp
from jax import lax
from jax.experimental import pallas as pl
from jax.experimental.pallas import tpu as pltpu
from jax.sharding import PartitionSpec as P

RING = 4
CORES = 2
BANDS = 4
STAGES = 2
STAT = 32
WIDTH = 1024
HALF = 512
COLS = 1024
ROWS = 256
BLOCK = 256
MESH = pl.DeviceIdType.MESH
OPP, PLUS, MINUS, OWN = 0, 1, 2, 3
ROW_SHIFT = (2, 1, 3, 0)


def wrap(value):
    return lax.rem(value + RING, RING)


def device(x, y, z, core):
    return (y * 2 + lax.rem(x, 2), lax.div(x, 2) * 8 + z * 2 + core)


def kernel(
    x_ref, bins_row, bins_col, table_ref, out_ref,
    ybuf, lbuf, d1buf, d2buf, dbuf, sbuf, pbuf, rs1, gbuf, fbuf,
    hop_send, q_send, half_send, bin_send, rs_send, fin_send,
    own_recv, p_recv, q_recv, x_recv, d_recv, rs_recv, f_recv,
):
    grp = lax.axis_index("grp")
    sub = lax.axis_index("sub")
    y, x_lo = lax.div(grp, 2), lax.rem(grp, 2)
    x_hi, z, c = lax.div(sub, 8), lax.rem(lax.div(sub, 2), RING), lax.rem(sub, 2)
    x = x_hi * 2 + x_lo
    other = 1 - c
    scale = 2.0 / math.sqrt(HALF)

    def place(yy, zz, k):
        return (yy * RING + zz) * CORES + k

    def flow(k, p, q):
        yy = wrap(y + (1 - k) * p + k * q)
        zz = wrap(z + k * p + (1 - k) * q)
        return yy, zz

    def slot(k, p, q):
        yy, zz = flow(k, p, q)
        return place(yy, zz, k)

    def start(src, dst, send, recv, target):
        pltpu.make_async_remote_copy(
            src_ref=src, dst_ref=dst, send_sem=send, recv_sem=recv,
            device_id=target, device_id_type=MESH,
        ).start()

    def await_bytes(ref, sem):
        pltpu.make_async_copy(ref, ref, sem).wait()

    barrier = pltpu.get_barrier_semaphore()
    chips = []
    for dx in (1, 2, 3):
        chips.append((wrap(x + dx), y, z))
    for dy in (1, 2, 3):
        chips.append((x, wrap(y + dy), z))
        chips.append((wrap(x + 2), wrap(y + dy), z))
    flip = x + 1 - 2 * x_lo
    for dz in (1, 2, 3):
        chips.append((x, y, wrap(z + dz)))
        chips.append((flip, y, wrap(z + dz)))
    pl.semaphore_signal(barrier, inc=1, device_id=device(x, y, z, other), device_id_type=MESH)
    for chip in chips:
        for core in range(CORES):
            pl.semaphore_signal(barrier, inc=1, device_id=device(*chip, core), device_id_type=MESH)
    pl.semaphore_wait(barrier, len(chips) * CORES + 1)

    def first_hop(t):
        here = slot(c, 0, 0)
        start(x_ref.at[2 * other + t], ybuf.at[t, here], hop_send.at[t], own_recv.at[t],
              device(x, y, z, other))
        for sign, index in ((1, 0), (-1, 1)):
            yy, zz = flow(c, sign, 0)
            for core in range(CORES):
                start(x_ref.at[2 * core + t], ybuf.at[t, here], hop_send.at[t],
                      p_recv.at[t, c, index], device(x, yy, zz, core))

    def first_rows(t):
        for sign, index, row in ((1, 0, MINUS), (-1, 1, PLUS)):
            for core in range(CORES):
                start(x_ref.at[2 * core + t], lbuf.at[t, 0, row, c], hop_send.at[t],
                      x_recv.at[t, c, index], device(wrap(x + sign), y, z, core))

    def q_out(t, k, p, p_index):
        here = slot(k, p, 0)
        for sign, index in ((1, 0), (-1, 1)):
            yy, zz = flow(k, 0, sign)
            start(ybuf.at[t, here], ybuf.at[t, here], q_send.at[t],
                  q_recv.at[t, k, p_index, index], device(x, yy, zz, c))

    def own_local(t):
        mine = x_ref[2 * c + t]
        ybuf[t, slot(c, 0, 0)] = mine
        lbuf[t, 0, OWN, c] = mine
        q_out(t, c, 0, 0)

    def own_remote(t):
        here = slot(other, 0, 0)
        await_bytes(ybuf.at[t, here], own_recv.at[t])
        q_out(t, other, 0, 0)
        lbuf[t, 0, OWN, other] = ybuf[t, here]

    def p_step(t):
        for sign, index in ((-1, 0), (1, 1)):
            for k in range(CORES):
                here = slot(k, sign, 0)
                await_bytes(ybuf.at[t, here], p_recv.at[t, k, index])
                q_out(t, k, sign, 1 + index)
                yy, zz = flow(k, -sign, 0)
                part = pl.ds(16 * index, 16)
                start(ybuf.at[t, here, part], ybuf.at[t, here, part], half_send.at[t],
                      p_recv.at[t, k, 2], device(x, yy, zz, c))

    def p_last(t):
        for k in range(CORES):
            await_bytes(ybuf.at[t, slot(k, 2, 0)], p_recv.at[t, k, 2])
            q_out(t, k, 2, 3)

    def x_step(t):
        for row, index, sign in ((MINUS, 0, 1), (PLUS, 1, -1)):
            for k in range(CORES):
                await_bytes(lbuf.at[t, 0, row, k], x_recv.at[t, k, index])
                part = pl.ds(16 * index, 16)
                start(lbuf.at[t, 0, row, k, part], lbuf.at[t, 0, OPP, k, part], half_send.at[t],
                      x_recv.at[t, k, 2], device(wrap(x + sign), y, z, c))

    def x_last(t):
        for k in range(CORES):
            await_bytes(lbuf.at[t, 0, OPP, k], x_recv.at[t, k, 2])
        for row in range(RING):
            for k in range(CORES):
                lbuf[t, 1, row, k, :, :HALF] = lbuf[t, 0, row, k, :, HALF:]
                lbuf[t, 1, row, k, :, HALF:] = -lbuf[t, 0, row, k, :, :HALF]

    SHIFT = (0, -1, 1, 2)

    def q_step(t, p_index):
        p = SHIFT[p_index]
        for sign, index in ((-1, 0), (1, 1)):
            for k in range(CORES):
                here = slot(k, p, sign)
                await_bytes(ybuf.at[t, here], q_recv.at[t, k, p_index, index])
                yy, zz = flow(k, 0, -sign)
                part = pl.ds(16 * index, 16)
                start(ybuf.at[t, here, part], ybuf.at[t, here, part], half_send.at[t],
                      q_recv.at[t, k, p_index, 2], device(x, yy, zz, c))

    def q_last(t, k, p_index):
        await_bytes(ybuf.at[t, slot(k, SHIFT[p_index], 2)], q_recv.at[t, k, p_index, 2])

    def send_bins():
        here = z * CORES + c
        for turn in range(2):
            for dz in range(RING):
                to_x = x if turn == 0 else flip
                to_lo = lax.rem(to_x, 2)
                to_z = wrap(z + dz)
                for core in range(CORES):
                    src = bins_row.at[to_lo, :, to_z]
                    dst = d1buf.at[here, :, x_lo]
                    if turn == 0 and dz == 0:
                        @pl.when(core == c)
                        def _():
                            pltpu.make_async_copy(src, dst, d_recv.at[0]).start()

                        @pl.when(core != c)
                        def _():
                            start(src, dst, bin_send.at[0], d_recv.at[0], device(to_x, y, to_z, core))
                    else:
                        start(src, dst, bin_send.at[0], d_recv.at[0], device(to_x, y, to_z, core))
        for turn in range(2):
            for dy in range(RING):
                to_hi = x_hi if turn == 0 else 1 - x_hi
                to_x = to_hi * 2 + x_lo
                to_y = wrap(y + dy)
                for core in range(CORES):
                    src = bins_col.at[to_hi, to_y]
                    dst = d2buf.at[y, x_hi, :, c]
                    if turn == 0 and dy == 0:
                        @pl.when(core == c)
                        def _():
                            pltpu.make_async_copy(src, dst, d_recv.at[1]).start()

                        @pl.when(core != c)
                        def _():
                            start(src, dst, bin_send.at[1], d_recv.at[1], device(to_x, to_y, z, core))
                    else:
                        start(src, dst, bin_send.at[1], d_recv.at[1], device(to_x, to_y, z, core))

    def wait_bins():
        await_bytes(d1buf, d_recv.at[0])
        await_bytes(d2buf, d_recv.at[1])

    def lookups():
        names = []
        for t in range(STAGES):
            for part in range(2):
                line = table_ref[pl.ds(BANDS * part + 2 * c + t, 1), :]
                names.append(jnp.broadcast_to(line, (64, 128)))

        def one_row(row, carry):
            rx = lax.rem(x + jnp.where(row == 0, 2, jnp.where(row == 1, 1, jnp.where(row == 2, 3, 0))), RING)
            rhi, rlo = lax.div(rx, 2), lax.rem(rx, 2)
            pieces = [d1buf[zk, rhi, rlo].astype(jnp.float32) for zk in range(8)]
            for yy in range(RING):
                mirrored = d2buf[yy, rhi, rlo].astype(jnp.float32).astype(jnp.int32).reshape(64, BLOCK)
                for side in range(2):
                    direct = jnp.concatenate(
                        [pieces[4 * side + i][:, yy * STAT:(yy + 1) * STAT] for i in range(4)], axis=1
                    ).astype(jnp.int32)
                    mirror = mirrored[:, side * 128:(side + 1) * 128]
                    for t in range(STAGES):
                        for part in range(2):
                            tab = names[2 * t + part]
                            one = jnp.take_along_axis(tab, direct, axis=1)
                            two = jnp.take_along_axis(tab, mirror, axis=1)
                            value = one + two if part == 0 else one - two
                            dbuf[t, part, row, :, pl.ds(yy * BLOCK + side * 128, 128)] = value
            return carry

        lax.fori_loop(0, RING, one_row, 0)

    def corr(t, dy):
        yy = wrap(y + dy)
        base = pl.multiple_of(yy * BLOCK, BLOCK)
        right = ybuf[t, pl.ds(yy * 8, 8)].reshape(BLOCK, WIDTH)
        for part in range(2):
            left = lbuf[t, part].reshape(ROWS, WIDTH)
            got = lax.dot_general(left, right, (((1,), (1,)), ((), ())),
                                  preferred_element_type=jnp.float32)
            value = got.reshape(RING, 64, BLOCK) * scale - dbuf[t, part, :, :, pl.ds(base, BLOCK)]
            sbuf[t, :, part, :, pl.ds(base, BLOCK)] = value.astype(jnp.bfloat16)

    def adjoint(t, half):
        left = sbuf[t, 2 * half:2 * half + 2].reshape(ROWS, COLS)
        for j in range(2):
            real = ybuf[t, :, :, j * 256:(j + 1) * 256].reshape(COLS, 256)
            imag = ybuf[t, :, :, HALF + j * 256:HALF + (j + 1) * 256].reshape(COLS, 256)
            a = jnp.dot(left, real, preferred_element_type=jnp.float32).reshape(2, 2, 64, 256)
            b = jnp.dot(left, imag, preferred_element_type=jnp.float32).reshape(2, 2, 64, 256)
            re = (a[:, 0] - b[:, 1]).reshape(2, CORES, STAT, 256)
            im = (b[:, 0] + a[:, 1]).reshape(2, CORES, STAT, 256)
            pbuf[t, 2 * half:2 * half + 2, :, :, j * 256:(j + 1) * 256] = re
            pbuf[t, 2 * half:2 * half + 2, :, :, HALF + j * 256:HALF + (j + 1) * 256] = im

    def sums_first(t):
        up, down = wrap(x + 1), wrap(x - 1)
        start(pbuf.at[t, OPP, 0], rs1.at[t, 0], rs_send.at[t], rs_recv.at[t, 0], device(up, y, z, c))
        start(pbuf.at[t, OPP, 1], rs1.at[t, 1], rs_send.at[t], rs_recv.at[t, 1], device(down, y, z, c))
        start(pbuf.at[t, PLUS, 1], fbuf.at[c, t, 0], rs_send.at[t], f_recv.at[c, t, 0], device(up, y, z, 1))

    def sums_second(t):
        down = wrap(x - 1)
        start(pbuf.at[t, MINUS, 0], fbuf.at[c, t, 1], rs_send.at[t], f_recv.at[c, t, 1], device(down, y, z, 0))
        start(pbuf.at[t, OWN, other], fbuf.at[c, t, 2], rs_send.at[t], f_recv.at[c, t, 2],
              device(x, y, z, other))

    def sums_forward(t):
        await_bytes(rs1.at[t, 0], rs_recv.at[t, 0])
        gbuf[t, 0] = rs1[t, 0] + pbuf[t, PLUS, 0]
        start(gbuf.at[t, 0], fbuf.at[c, t, 0], fin_send.at[t], f_recv.at[c, t, 0],
              device(wrap(x + 1), y, z, 0))
        await_bytes(rs1.at[t, 1], rs_recv.at[t, 1])
        gbuf[t, 1] = rs1[t, 1] + pbuf[t, MINUS, 1]
        start(gbuf.at[t, 1], fbuf.at[c, t, 1], fin_send.at[t], f_recv.at[c, t, 1],
              device(wrap(x - 1), y, z, 1))

    def sums_last(t):
        total = 1.0 / math.sqrt(COLS * RING)
        for i in range(2):
            await_bytes(fbuf.at[c, t, i], f_recv.at[c, t, i])
        out_ref[2 * c + t] = (fbuf[c, t, 0] + fbuf[c, t, 1] + pbuf[t, OWN, c]) * total
        for i in range(3):
            await_bytes(fbuf.at[other, t, i], f_recv.at[other, t, i])
        out_ref[2 * other + t] = (fbuf[other, t, 0] + fbuf[other, t, 1] + fbuf[other, t, 2]) * total

    def sends_done(t):
        await_bytes(ybuf.at[t, pl.ds(0, 9)], hop_send.at[t])
        await_bytes(ybuf.at[t, pl.ds(0, 16)], q_send.at[t])
        await_bytes(ybuf.at[t, pl.ds(0, 12)], half_send.at[t])

    first_hop(0)
    own_local(0)
    own_remote(0)
    first_rows(0)
    send_bins()
    p_step(0)
    x_step(0)
    p_last(0)
    first_hop(1)
    first_rows(1)
    q_step(0, 0)
    own_local(1)
    own_remote(1)
    p_step(1)
    x_step(1)
    wait_bins()
    lookups()
    x_last(0)
    q_step(0, 1)
    q_step(0, 2)
    p_last(1)
    q_last(0, 0, 0)
    corr(0, 0)
    q_step(0, 3)
    x_last(1)
    q_last(0, 0, 2)
    corr(0, 1)
    q_last(0, 0, 1)
    corr(0, -1)
    q_step(1, 0)
    q_last(0, 0, 3)
    for i in range(4):
        q_last(0, 1, i)
    corr(0, 2)
    adjoint(0, 0)
    sums_first(0)
    q_step(1, 1)
    q_step(1, 2)
    adjoint(0, 1)
    sums_second(0)
    q_last(1, 0, 0)
    corr(1, 0)
    sums_forward(0)
    q_step(1, 3)
    q_last(1, 0, 2)
    corr(1, 1)
    q_last(1, 0, 1)
    corr(1, -1)
    sends_done(0)
    for i in range(2):
        await_bytes(ybuf.at[0, pl.ds(0, 15), pl.ds(0, 16)], bin_send.at[i])
    q_last(1, 0, 3)
    for i in range(4):
        q_last(1, 1, i)
    corr(1, 2)
    adjoint(1, 0)
    sums_first(1)
    adjoint(1, 1)
    sums_second(1)
    sums_forward(1)
    sums_last(0)
    sends_done(1)
    sums_last(1)
    for t in range(STAGES):
        await_bytes(ybuf.at[t, pl.ds(0, 10)], rs_send.at[t])
        await_bytes(gbuf.at[t], fin_send.at[t])


def exchange(spectra, bins_row, bins_col, table):
    f32, bf16 = jnp.float32, jnp.bfloat16
    dma = pltpu.SemaphoreType.DMA
    vmem = pl.BlockSpec(memory_space=pltpu.VMEM)
    return pl.pallas_call(
        kernel,
        out_shape=jax.ShapeDtypeStruct((BANDS, STAT, WIDTH), f32),
        in_specs=[vmem] * 4,
        out_specs=vmem,
        scratch_shapes=[
            pltpu.VMEM((STAGES, 32, STAT, WIDTH), bf16),
            pltpu.VMEM((STAGES, 2, RING, CORES, STAT, WIDTH), bf16),
            pltpu.VMEM((8, 2, 2, 64, 128), bf16),
            pltpu.VMEM((RING, 2, 2, CORES, STAT, BLOCK), bf16),
            pltpu.VMEM((STAGES, 2, RING, 64, COLS), f32),
            pltpu.VMEM((STAGES, RING, 2, 64, COLS), bf16),
            pltpu.VMEM((STAGES, RING, CORES, STAT, WIDTH), f32),
            pltpu.VMEM((STAGES, 2, STAT, WIDTH), f32),
            pltpu.VMEM((STAGES, 2, STAT, WIDTH), f32),
            pltpu.VMEM((CORES, STAGES, 3, STAT, WIDTH), f32),
            dma((STAGES,)), dma((STAGES,)), dma((STAGES,)), dma((2,)), dma((STAGES,)), dma((STAGES,)),
            dma((STAGES,)), dma((STAGES, CORES, 3)), dma((STAGES, CORES, 4, 3)),
            dma((STAGES, CORES, 3)), dma((2,)), dma((STAGES, 2)), dma((CORES, STAGES, 3)),
        ],
        compiler_params=pltpu.CompilerParams(
            collective_id=0, has_side_effects=True, vmem_limit_bytes=48 * 1024 * 1024
        ),
    )(spectra, bins_row, bins_col, table)


def per_device(records, ref_bin, ref_table):
    spectra = records.reshape(STAT, 2, BANDS, HALF).transpose(2, 0, 1, 3).reshape(BANDS, STAT, WIDTH)
    tile = ref_bin[0, :, 0, :].astype(jnp.bfloat16)
    bins_row = tile.reshape(2, RING, 64, RING, 2, STAT).transpose(4, 0, 1, 2, 3, 5)
    bins_row = bins_row.reshape(2, 2, RING, 64, 128)
    bins_col = tile.reshape(2, BLOCK, RING, 2, STAT).transpose(0, 2, 3, 4, 1)
    table = jnp.pad(ref_table.astype(jnp.float32).T, ((0, 0), (0, 64)))
    out = exchange(spectra, bins_row, bins_col, table)
    return out.reshape(BANDS, STAT, 2, HALF).transpose(1, 2, 0, 3).reshape(STAT, 2, BANDS * HALF)


def solution(mesh):
    in_specs = (P(("grp", "sub"), None, None), P("grp", None, "sub", None), P())
    out_specs = P(("grp", "sub"), None, None)
    return jax.shard_map(
        per_device, mesh=mesh, in_specs=in_specs, out_specs=out_specs, check_vma=False
    )
```

```python
import math

import jax
import jax.numpy as jnp
from jax import lax
from jax.experimental import pallas as pl
from jax.experimental.pallas import tpu as pltpu
from jax.sharding import PartitionSpec as P

RING = 4
CORES = 2
BANDS = 4
STAGES = 2
STAT = 32
WIDTH = 1024
HALF = 512
COLS = 1024
ROWS = 256
BLOCK = 256
MESH = pl.DeviceIdType.MESH
OPP, PLUS, MINUS, OWN = 0, 1, 2, 3
ROW_SHIFT = (2, 1, 3, 0)


def wrap(value):
    return lax.rem(value + RING, RING)


def device(x, y, z, core):
    return (y * 2 + lax.rem(x, 2), lax.div(x, 2) * 8 + z * 2 + core)


def kernel(
    raw_x, raw_bins, raw_table, out_ref,
    xraw, xwide, xbuf, braw, table, brow, bcol,
    ybuf, lbuf, d1buf, d2buf, dbuf, sbuf, pbuf, hbuf, rs1, gbuf, fbuf, nbuf,
    in_sem, hop_send, q_send, half_send, bin_send, rs_send, fin_send, own_send,
    own_recv, p_recv, q_recv, x_recv, d_recv, rs_recv, f_recv, n_recv,
):
    grp = lax.axis_index("grp")
    sub = lax.axis_index("sub")
    y, x_lo = lax.div(grp, 2), lax.rem(grp, 2)
    x_hi, z, c = lax.div(sub, 8), lax.rem(lax.div(sub, 2), RING), lax.rem(sub, 2)
    x = x_hi * 2 + x_lo
    other = 1 - c
    flip = x + 1 - 2 * x_lo
    scale = 2.0 / math.sqrt(HALF)
    f32, bf16 = jnp.float32, jnp.bfloat16

    def flow(k, p, q):
        yy = wrap(y + (1 - k) * p + k * q)
        zz = wrap(z + k * p + (1 - k) * q)
        return yy, zz

    def slot(k, p, q):
        yy, zz = flow(k, p, q)
        return (yy * RING + zz) * CORES + k

    def start(src, dst, send, recv, target):
        pltpu.make_async_remote_copy(
            src_ref=src, dst_ref=dst, send_sem=send, recv_sem=recv,
            device_id=target, device_id_type=MESH,
        ).start()

    def await_bytes(ref, sem):
        pltpu.make_async_copy(ref, ref, sem).wait()

    loads = [
        pltpu.make_async_copy(raw_x, xraw, in_sem.at[0]),
        pltpu.make_async_copy(raw_bins, braw, in_sem.at[1]),
        pltpu.make_async_copy(raw_table, table.at[0], in_sem.at[2]),
    ]
    for load in loads:
        load.start()
    barrier = pltpu.get_barrier_semaphore()
    near = [(wrap(x + d), y, z) for d in (1, 3)]
    near += [(x, wrap(y + d), z) for d in (1, 3)]
    near += [(x, y, wrap(z + d)) for d in (1, 3)]
    far = [(wrap(x + 2), wrap(y + d), z) for d in range(RING)] + [(x, wrap(y + 2), z)]
    far += [(flip, y, wrap(z + d)) for d in (1, 2, 3)] + [(x, y, wrap(z + 2))]
    peers = [device(x, y, z, other)] + [device(*chip, c) for chip in near + far]
    peers += [device(*chip, other) for chip in near]
    for peer in peers:
        pl.semaphore_signal(barrier, inc=1, device_id=peer, device_id_type=MESH)

    loads[0].wait()
    xwide[...] = xraw[...].astype(f32)
    for band in range(BANDS):
        for part in range(2):
            for j in range(4):
                line = xwide[pl.ds((band * 4 + j) * 2 + part, STAT, stride=32), :]
                xbuf[band, :, part * HALF + j * 128:part * HALF + (j + 1) * 128] = line.astype(bf16)
    pl.semaphore_wait(barrier, len(peers))

    def first_hop(t):
        here = slot(c, 0, 0)
        for index, sign in ((0, 1), (1, -1)):
            yy, zz = flow(c, sign, 0)
            for core in range(CORES):
                start(xbuf.at[2 * core + t], ybuf.at[t, here], hop_send.at[t],
                      p_recv.at[t, c, index], device(x, yy, zz, core))
        for index, sign in ((0, 1), (1, -1)):
            yy, zz = flow(c, 0, sign)
            for core in range(CORES):
                start(xbuf.at[2 * core + t], ybuf.at[t, here], hop_send.at[t],
                      q_recv.at[t, c, 0, index], device(x, yy, zz, core))
        start(xbuf.at[2 * other + t], ybuf.at[t, here], hop_send.at[t], own_recv.at[t],
              device(x, y, z, other))
        for sign, index, row in ((1, 0, MINUS), (-1, 1, PLUS)):
            for core in range(CORES):
                start(xbuf.at[2 * core + t], lbuf.at[t, 0, row, c], hop_send.at[t],
                      x_recv.at[t, c, index], device(wrap(x + sign), y, z, core))

    def own_units(t):
        mine = xbuf[2 * c + t]
        ybuf[t, slot(c, 0, 0)] = mine
        lbuf[t, 0, OWN, c] = mine
        here = slot(other, 0, 0)
        await_bytes(ybuf.at[t, here], own_recv.at[t])
        lbuf[t, 0, OWN, other] = ybuf[t, here]

    SHIFT = (0, -1, 1, 2)

    def q_out(t, k, p_index):
        here = slot(k, SHIFT[p_index], 0)
        for sign, index in ((1, 0), (-1, 1)):
            yy, zz = flow(k, 0, sign)
            start(ybuf.at[t, here], ybuf.at[t, here], q_send.at[t],
                  q_recv.at[t, k, p_index, index], device(x, yy, zz, c))

    def p_step(t):
        for sign, index in ((-1, 0), (1, 1)):
            for k in range(CORES):
                here = slot(k, sign, 0)
                await_bytes(ybuf.at[t, here], p_recv.at[t, k, index])
                yy, zz = flow(k, -sign, 0)
                part = pl.ds(16 * index, 16)
                start(ybuf.at[t, here, part], ybuf.at[t, here, part], half_send.at[t],
                      p_recv.at[t, k, 2], device(x, yy, zz, c))

    def q_near(t):
        for p_index in (1, 2):
            for k in range(CORES):
                q_out(t, k, p_index)

    def p_last(t):
        for k in range(CORES):
            await_bytes(ybuf.at[t, slot(k, 2, 0)], p_recv.at[t, k, 2])
            q_out(t, k, 3)

    def x_step(t):
        for row, index, sign in ((MINUS, 0, 1), (PLUS, 1, -1)):
            for k in range(CORES):
                await_bytes(lbuf.at[t, 0, row, k], x_recv.at[t, k, index])
                part = pl.ds(16 * index, 16)
                start(lbuf.at[t, 0, row, k, part], lbuf.at[t, 0, OPP, k, part], half_send.at[t],
                      x_recv.at[t, k, 2], device(wrap(x + sign), y, z, c))

    def x_last(t):
        for k in range(CORES):
            await_bytes(lbuf.at[t, 0, OPP, k], x_recv.at[t, k, 2])
        for row in range(RING):
            for k in range(CORES):
                lbuf[t, 1, row, k, :, :HALF] = lbuf[t, 0, row, k, :, HALF:]
                lbuf[t, 1, row, k, :, HALF:] = -lbuf[t, 0, row, k, :, :HALF]

    def q_step(t, p_index):
        p = SHIFT[p_index]
        for sign, index in ((-1, 0), (1, 1)):
            for k in range(CORES):
                here = slot(k, p, sign)
                await_bytes(ybuf.at[t, here], q_recv.at[t, k, p_index, index])
                yy, zz = flow(k, 0, -sign)
                part = pl.ds(16 * index, 16)
                start(ybuf.at[t, here, part], ybuf.at[t, here, part], half_send.at[t],
                      q_recv.at[t, k, p_index, 2], device(x, yy, zz, c))

    def q_last(t, k, p_index):
        await_bytes(ybuf.at[t, slot(k, SHIFT[p_index], 2)], q_recv.at[t, k, p_index, 2])

    def make_bins():
        loads[1].wait()
        tile = jnp.concatenate(
            [braw[pl.ds(h, 512, stride=2), :].astype(f32).astype(bf16) for h in range(2)], axis=1
        )
        source = lax.broadcasted_iota(jnp.int32, (BLOCK, BLOCK), 0)
        column = lax.broadcasted_iota(jnp.int32, (BLOCK, BLOCK), 1)
        wanted = ((column // 32) % 4) * 64 + (column // 128) * 32 + column % 32
        order = (source == wanted).astype(bf16)
        same = (source == column).astype(bf16)
        by_row = jnp.dot(tile, order, preferred_element_type=f32).astype(bf16)
        for lo in range(2):
            brow[lo] = by_row[:, lo * 128:(lo + 1) * 128].reshape(2, RING, 64, 128)
        by_col = lax.dot_general(same, tile, (((1,), (1,)), ((), ())),
                                 preferred_element_type=f32).astype(bf16)
        for hi in range(2):
            bcol[hi] = by_col[:, hi * BLOCK:(hi + 1) * BLOCK].reshape(RING, 2, STAT, BLOCK)

    def send_bins():
        for turn in range(2):
            to_x = x if turn == 0 else flip
            to_lo = lax.rem(to_x, 2)
            for dz in range(RING):
                to_z = wrap(z + dz)
                src, dst = brow.at[to_lo, :, to_z], d1buf.at[c, z, :, x_lo]
                if turn == 0 and dz == 0:
                    pltpu.make_async_copy(src, dst, d_recv.at[0]).start()
                else:
                    start(src, dst, bin_send.at[0], d_recv.at[0], device(to_x, y, to_z, c))
        for turn in range(2):
            to_hi = x_hi if turn == 0 else 1 - x_hi
            for dy in range(RING):
                to_y = wrap(y + dy)
                src, dst = bcol.at[to_hi, to_y], d2buf.at[c, y, x_hi]
                if turn == 0 and dy == 0:
                    pltpu.make_async_copy(src, dst, d_recv.at[1]).start()
                else:
                    start(src, dst, bin_send.at[1], d_recv.at[1], device(to_hi * 2 + x_lo, to_y, z, c))

    def share_bins():
        await_bytes(d1buf.at[c], d_recv.at[0])
        start(d1buf.at[c], d1buf.at[c], bin_send.at[2], d_recv.at[2], device(x, y, z, other))
        await_bytes(d2buf.at[c], d_recv.at[1])
        start(d2buf.at[c], d2buf.at[c], bin_send.at[2], d_recv.at[3], device(x, y, z, other))

    def wait_bins():
        await_bytes(d1buf.at[other], d_recv.at[2])
        await_bytes(d2buf.at[other], d_recv.at[3])
        loads[2].wait()
        table[1] = table[0]

    def lookups(row):
        wide = jnp.concatenate([table[0], table[1]], axis=1).astype(f32)
        table_wide = wide
        names = []
        for t in range(STAGES):
            for part in range(2):
                line = table_line(table_wide, BANDS * part, t)
                names.append(jnp.broadcast_to(line, (64, 128)))
        rx = wrap(x + ROW_SHIFT[row])
        rhi, rlo = lax.div(rx, 2), lax.rem(rx, 2)
        pieces = [d1buf[k, zz, rhi, rlo].astype(f32) for zz in range(RING) for k in range(CORES)]
        for yy in range(RING):
            mirrored = d2buf[:, yy, rhi, rlo].astype(f32).astype(jnp.int32).reshape(64, BLOCK)
            for side in range(2):
                direct = jnp.concatenate(
                    [pieces[4 * side + i][:, yy * STAT:(yy + 1) * STAT] for i in range(4)], axis=1
                ).astype(jnp.int32)
                mirror = mirrored[:, side * 128:(side + 1) * 128]
                for t in range(STAGES):
                    for part in range(2):
                        tab = names[2 * t + part]
                        one = jnp.take_along_axis(tab, direct, axis=1)
                        two = jnp.take_along_axis(tab, mirror, axis=1)
                        value = one + two if part == 0 else one - two
                        dbuf[t, part, row, :, pl.ds(yy * BLOCK + side * 128, 128)] = value

    def table_line(wide, base, t):
        return jnp.where(c == 0, wide[base + t:base + t + 1], wide[base + 2 + t:base + 3 + t])

    def corr(t, dy):
        yy = wrap(y + dy)
        base = pl.multiple_of(yy * BLOCK, BLOCK)
        right = ybuf[t, pl.ds(yy * 8, 8)].reshape(BLOCK, WIDTH)
        for part in range(2):
            left = lbuf[t, part].reshape(ROWS, WIDTH)
            got = lax.dot_general(left, right, (((1,), (1,)), ((), ())), preferred_element_type=f32)
            value = got.reshape(RING, 64, BLOCK) * scale - dbuf[t, part, :, :, pl.ds(base, BLOCK)]
            sbuf[t, :, part, :, pl.ds(base, BLOCK)] = value.astype(bf16)

    def adjoint(t, half):
        left = sbuf[t, 2 * half:2 * half + 2].reshape(ROWS, COLS)
        for j in range(2):
            real = ybuf[t, :, :, j * 256:(j + 1) * 256].reshape(COLS, 256)
            imag = ybuf[t, :, :, HALF + j * 256:HALF + (j + 1) * 256].reshape(COLS, 256)
            a = jnp.dot(left, real, preferred_element_type=f32).reshape(2, 2, 64, 256)
            b = jnp.dot(left, imag, preferred_element_type=f32).reshape(2, 2, 64, 256)
            re = (a[:, 0] - b[:, 1]).reshape(2, CORES, STAT, 256)
            im = (b[:, 0] + a[:, 1]).reshape(2, CORES, STAT, 256)
            for value, base in ((re, j * 256), (im, HALF + j * 256)):
                pbuf[t, 2 * half:2 * half + 2, :, :, base:base + 256] = value
                hbuf[t, 2 * half:2 * half + 2, :, :, base:base + 256] = value.astype(bf16)

    def sums_first(t):
        up, down = wrap(x + 1), wrap(x - 1)
        start(hbuf.at[t, OPP, 0], rs1.at[t, 0], rs_send.at[t], rs_recv.at[t, 0], device(up, y, z, c))
        start(hbuf.at[t, OPP, 1], rs1.at[t, 1], rs_send.at[t], rs_recv.at[t, 1], device(down, y, z, c))
        start(hbuf.at[t, PLUS, 1], fbuf.at[c, t, 0], rs_send.at[t], f_recv.at[c, t, 0], device(up, y, z, 1))

    def sums_second(t):
        down = wrap(x - 1)
        start(hbuf.at[t, MINUS, 0], fbuf.at[c, t, 1], rs_send.at[t], f_recv.at[c, t, 1], device(down, y, z, 0))
        start(pbuf.at[t, OWN, other], nbuf.at[t], own_send.at[t], n_recv.at[t], device(x, y, z, other))

    def sums_forward(t):
        await_bytes(rs1.at[t, 0], rs_recv.at[t, 0])
        gbuf[t, 0] = (rs1[t, 0].astype(f32) + pbuf[t, PLUS, 0]).astype(bf16)
        start(gbuf.at[t, 0], fbuf.at[c, t, 0], fin_send.at[t], f_recv.at[c, t, 0],
              device(wrap(x + 1), y, z, 0))
        await_bytes(rs1.at[t, 1], rs_recv.at[t, 1])
        gbuf[t, 1] = (rs1[t, 1].astype(f32) + pbuf[t, MINUS, 1]).astype(bf16)
        start(gbuf.at[t, 1], fbuf.at[c, t, 1], fin_send.at[t], f_recv.at[c, t, 1],
              device(wrap(x - 1), y, z, 1))

    def store(band, value):
        value = value * (1.0 / math.sqrt(COLS * RING))
        for part in range(2):
            for j in range(4):
                piece = value[:, part * HALF + j * 128:part * HALF + (j + 1) * 128]
                out_ref[pl.ds(band * 8 + j * 2 + part, STAT, stride=32), :] = piece

    def sums_last(t):
        await_bytes(nbuf.at[t], n_recv.at[t])
        for core, mine in ((other, nbuf.at[t]), (c, pbuf.at[t, OWN, c])):
            for i in range(2):
                await_bytes(fbuf.at[core, t, i], f_recv.at[core, t, i])
            store(2 * core + t, mine[...] + fbuf[core, t, 0].astype(f32) + fbuf[core, t, 1].astype(f32))

    def sends_done(t):
        await_bytes(ybuf.at[t, pl.ds(0, 13)], hop_send.at[t])
        await_bytes(ybuf.at[t, pl.ds(0, 12)], q_send.at[t])
        await_bytes(ybuf.at[t, pl.ds(0, 12)], half_send.at[t])

    first_hop(0)
    first_hop(1)
    make_bins()
    send_bins()
    p_step(0)
    q_near(0)
    x_step(0)
    own_units(0)
    q_step(0, 0)
    p_step(1)
    x_step(1)
    own_units(1)
    share_bins()
    p_last(0)
    x_last(0)
    wait_bins()
    lookups(0)
    q_step(0, 1)
    q_step(0, 2)
    q_near(1)
    lookups(1)
    q_step(1, 0)
    q_step(0, 3)
    p_last(1)
    lookups(2)
    lookups(3)
    q_last(0, 0, 0)
    corr(0, 0)
    x_last(1)
    q_last(0, 0, 2)
    corr(0, 1)
    q_step(1, 1)
    q_step(1, 2)
    q_last(0, 0, 1)
    corr(0, -1)
    q_last(0, 0, 3)
    for i in range(4):
        q_last(0, 1, i)
    corr(0, 2)
    q_step(1, 3)
    adjoint(0, 0)
    sums_first(0)
    adjoint(0, 1)
    sums_second(0)
    q_last(1, 0, 0)
    corr(1, 0)
    sends_done(0)
    for i in range(2):
        await_bytes(ybuf.at[0, pl.ds(0, 7), pl.ds(0, 16)], bin_send.at[i])
    await_bytes(ybuf.at[0, pl.ds(0, 8)], bin_send.at[2])
    q_last(1, 0, 2)
    corr(1, 1)
    q_last(1, 0, 1)
    corr(1, -1)
    sums_forward(0)
    q_last(1, 0, 3)
    for i in range(4):
        q_last(1, 1, i)
    corr(1, 2)
    adjoint(1, 0)
    sums_first(1)
    adjoint(1, 1)
    sums_second(1)
    sums_last(0)
    sums_forward(1)
    sends_done(1)
    await_bytes(hbuf.at[0, pl.ds(0, 2)], rs_send.at[0])
    await_bytes(nbuf.at[0], own_send.at[0])
    await_bytes(gbuf.at[0], fin_send.at[0])
    sums_last(1)
    await_bytes(hbuf.at[1, pl.ds(0, 2)], rs_send.at[1])
    await_bytes(nbuf.at[1], own_send.at[1])
    await_bytes(gbuf.at[1], fin_send.at[1])


def exchange(spectra, bins, table):
    f32, bf16, i32 = jnp.float32, jnp.bfloat16, jnp.int32
    dma, vmem = pltpu.SemaphoreType.DMA, pltpu.VMEM
    return pl.pallas_call(
        kernel,
        out_shape=jax.ShapeDtypeStruct((STAT * 32, 128), f32),
        in_specs=[pl.BlockSpec(memory_space=pltpu.HBM)] * 3,
        out_specs=pl.BlockSpec(memory_space=pltpu.VMEM),
        scratch_shapes=[
            vmem((STAT * 32, 128), bf16),
            vmem((STAT * 32, 128), f32),
            vmem((BANDS, STAT, WIDTH), bf16),
            vmem((1024, 128), i32),
            vmem((2, 2 * BANDS, 64), bf16),
            vmem((2, 2, RING, 64, 128), bf16),
            vmem((2, RING, 2, STAT, BLOCK), bf16),
            vmem((STAGES, 32, STAT, WIDTH), bf16),
            vmem((STAGES, 2, RING, CORES, STAT, WIDTH), bf16),
            vmem((CORES, RING, 2, 2, 64, 128), bf16),
            vmem((CORES, RING, 2, 2, STAT, BLOCK), bf16),
            vmem((STAGES, 2, RING, 64, COLS), f32),
            vmem((STAGES, RING, 2, 64, COLS), bf16),
            vmem((STAGES, RING, CORES, STAT, WIDTH), f32),
            vmem((STAGES, RING, CORES, STAT, WIDTH), bf16),
            vmem((STAGES, 2, STAT, WIDTH), bf16),
            vmem((STAGES, 2, STAT, WIDTH), bf16),
            vmem((CORES, STAGES, 2, STAT, WIDTH), bf16),
            vmem((STAGES, STAT, WIDTH), f32),
            dma((3,)), dma((STAGES,)), dma((STAGES,)), dma((STAGES,)), dma((3,)), dma((STAGES,)),
            dma((STAGES,)), dma((STAGES,)), dma((STAGES,)), dma((STAGES, CORES, 3)), dma((STAGES, CORES, 4, 3)),
            dma((STAGES, CORES, 3)), dma((4,)), dma((STAGES, 2)), dma((CORES, STAGES, 2)), dma((STAGES,)),
        ],
        compiler_params=pltpu.CompilerParams(
            collective_id=0, has_side_effects=True, vmem_limit_bytes=48 * 1024 * 1024
        ),
    )(spectra, bins, table)


def per_device(records, ref_bin, ref_table):
    spectra = records.reshape(STAT, 2, 16, 128).transpose(0, 2, 1, 3).reshape(STAT * 32, 128)
    args = (spectra, ref_bin.reshape(1024, 128), ref_table.T)
    out = exchange(*(pltpu.with_memory_space_constraint(arg, pltpu.HBM) for arg in args))
    return out.reshape(STAT, 16, 2, 128).transpose(0, 2, 1, 3).reshape(STAT, 2, 2048)


def solution(mesh):
    in_specs = (P(("grp", "sub"), None, None), P("grp", None, "sub", None), P())
    out_specs = P(("grp", "sub"), None, None)
    return jax.shard_map(
        per_device, mesh=mesh, in_specs=in_specs, out_specs=out_specs, check_vma=False
    )
```

```python
import math

import jax
import jax.numpy as jnp
from jax import lax
from jax.experimental import pallas as pl
from jax.experimental.pallas import tpu as pltpu
from jax.sharding import PartitionSpec as P

RING = 4
CORES = 2
BANDS = 4
STAGES = 2
STAT = 32
WIDTH = 1024
HALF = 512
COLS = 1024
ROWS = 256
BLOCK = 256
MESH = pl.DeviceIdType.MESH
OPP, PLUS, MINUS, OWN = 0, 1, 2, 3
ROW_SHIFT = (2, 1, 3, 0)


def wrap(value):
    return lax.rem(value + RING, RING)


def device(x, y, z, core):
    return (y * 2 + lax.rem(x, 2), lax.div(x, 2) * 8 + z * 2 + core)


def kernel(
    raw_x, raw_bins, raw_table, out_ref,
    xraw, xwide, xbuf, braw, table, brow, bcol,
    ybuf, lbuf, d1buf, d2buf, dbuf, sbuf, pbuf, hbuf, rs1, gbuf, fbuf, nbuf,
    in_sem, hop_send, q_send, half_send, bin_send, rs_send, fin_send, own_send,
    own_recv, p_recv, q_recv, x_recv, d_recv, rs_recv, f_recv, n_recv,
):
    grp = lax.axis_index("grp")
    sub = lax.axis_index("sub")
    y, x_lo = lax.div(grp, 2), lax.rem(grp, 2)
    x_hi, z, c = lax.div(sub, 8), lax.rem(lax.div(sub, 2), RING), lax.rem(sub, 2)
    x = x_hi * 2 + x_lo
    other = 1 - c
    flip = x + 1 - 2 * x_lo
    scale = 2.0 / math.sqrt(HALF)
    f32, bf16 = jnp.float32, jnp.bfloat16

    def flow(k, p, q):
        yy = wrap(y + (1 - k) * p + k * q)
        zz = wrap(z + k * p + (1 - k) * q)
        return yy, zz

    def slot(k, p, q):
        yy, zz = flow(k, p, q)
        return (yy * RING + zz) * CORES + k

    def start(src, dst, send, recv, target):
        pltpu.make_async_remote_copy(
            src_ref=src, dst_ref=dst, send_sem=send, recv_sem=recv,
            device_id=target, device_id_type=MESH,
        ).start()

    def await_bytes(ref, sem):
        pltpu.make_async_copy(ref, ref, sem).wait()

    loads = [
        pltpu.make_async_copy(raw_x, xraw, in_sem.at[0]),
        pltpu.make_async_copy(raw_bins, braw, in_sem.at[1]),
        pltpu.make_async_copy(raw_table, table.at[0], in_sem.at[2]),
    ]
    for load in loads:
        load.start()
    barrier = pltpu.get_barrier_semaphore()
    near = [(wrap(x + d), y, z) for d in (1, 3)]
    near += [(x, wrap(y + d), z) for d in (1, 3)]
    near += [(x, y, wrap(z + d)) for d in (1, 3)]
    far = [(wrap(x + 2), wrap(y + d), z) for d in range(RING)] + [(x, wrap(y + 2), z)]
    far += [(flip, y, wrap(z + d)) for d in (1, 2, 3)] + [(x, y, wrap(z + 2))]
    peers = [device(x, y, z, other)] + [device(*chip, c) for chip in near + far]
    peers += [device(*chip, other) for chip in near]
    for peer in peers:
        pl.semaphore_signal(barrier, inc=1, device_id=peer, device_id_type=MESH)

    loads[0].wait()
    xwide[...] = xraw[...].astype(f32)
    for band in range(BANDS):
        for part in range(2):
            for j in range(4):
                line = xwide[pl.ds((band * 4 + j) * 2 + part, STAT, stride=32), :]
                xbuf[band, :, part * HALF + j * 128:part * HALF + (j + 1) * 128] = line.astype(bf16)
    pl.semaphore_wait(barrier, len(peers))

    def hop_p(t):
        here = slot(c, 0, 0)
        for index, sign in ((0, 1), (1, -1)):
            yy, zz = flow(c, sign, 0)
            for core in range(CORES):
                start(xbuf.at[2 * core + t], ybuf.at[t, here], hop_send.at[t],
                      p_recv.at[t, c, index], device(x, yy, zz, core))

    def hop_q(t):
        here = slot(c, 0, 0)
        for index, sign in ((0, 1), (1, -1)):
            yy, zz = flow(c, 0, sign)
            for core in range(CORES):
                start(xbuf.at[2 * core + t], ybuf.at[t, here], hop_send.at[t],
                      q_recv.at[t, c, 0, index], device(x, yy, zz, core))

    def hop_x(t):
        start(xbuf.at[2 * other + t], ybuf.at[t, slot(c, 0, 0)], hop_send.at[t], own_recv.at[t],
              device(x, y, z, other))
        for sign, index, row in ((1, 0, MINUS), (-1, 1, PLUS)):
            for core in range(CORES):
                start(xbuf.at[2 * core + t], lbuf.at[t, 0, row, c], hop_send.at[t],
                      x_recv.at[t, c, index], device(wrap(x + sign), y, z, core))

    def own_units(t):
        mine = xbuf[2 * c + t]
        ybuf[t, slot(c, 0, 0)] = mine
        lbuf[t, 0, OWN, c] = mine
        here = slot(other, 0, 0)
        await_bytes(ybuf.at[t, here], own_recv.at[t])
        lbuf[t, 0, OWN, other] = ybuf[t, here]

    SHIFT = (0, -1, 1, 2)

    def q_out(t, k, p_index):
        here = slot(k, SHIFT[p_index], 0)
        for sign, index in ((1, 0), (-1, 1)):
            yy, zz = flow(k, 0, sign)
            start(ybuf.at[t, here], ybuf.at[t, here], q_send.at[t],
                  q_recv.at[t, k, p_index, index], device(x, yy, zz, c))

    def p_step(t):
        for sign, index in ((-1, 0), (1, 1)):
            for k in range(CORES):
                here = slot(k, sign, 0)
                await_bytes(ybuf.at[t, here], p_recv.at[t, k, index])
                yy, zz = flow(k, -sign, 0)
                part = pl.ds(16 * index, 16)
                start(ybuf.at[t, here, part], ybuf.at[t, here, part], half_send.at[t],
                      p_recv.at[t, k, 2], device(x, yy, zz, c))

    def q_near(t):
        for p_index in (1, 2):
            for k in range(CORES):
                q_out(t, k, p_index)

    def p_last(t):
        for k in range(CORES):
            await_bytes(ybuf.at[t, slot(k, 2, 0)], p_recv.at[t, k, 2])
            q_out(t, k, 3)

    def x_step(t):
        for row, index, sign in ((MINUS, 0, 1), (PLUS, 1, -1)):
            for k in range(CORES):
                await_bytes(lbuf.at[t, 0, row, k], x_recv.at[t, k, index])
                part = pl.ds(16 * index, 16)
                start(lbuf.at[t, 0, row, k, part], lbuf.at[t, 0, OPP, k, part], half_send.at[t],
                      x_recv.at[t, k, 2], device(wrap(x + sign), y, z, c))

    def x_last(t):
        for k in range(CORES):
            await_bytes(lbuf.at[t, 0, OPP, k], x_recv.at[t, k, 2])
        for row in range(RING):
            for k in range(CORES):
                lbuf[t, 1, row, k, :, :HALF] = lbuf[t, 0, row, k, :, HALF:]
                lbuf[t, 1, row, k, :, HALF:] = -lbuf[t, 0, row, k, :, :HALF]

    def q_step(t, p_index):
        p = SHIFT[p_index]
        for sign, index in ((-1, 0), (1, 1)):
            for k in range(CORES):
                here = slot(k, p, sign)
                await_bytes(ybuf.at[t, here], q_recv.at[t, k, p_index, index])
                yy, zz = flow(k, 0, -sign)
                part = pl.ds(16 * index, 16)
                start(ybuf.at[t, here, part], ybuf.at[t, here, part], half_send.at[t],
                      q_recv.at[t, k, p_index, 2], device(x, yy, zz, c))

    def q_last(t, k, p_index):
        await_bytes(ybuf.at[t, slot(k, SHIFT[p_index], 2)], q_recv.at[t, k, p_index, 2])

    def make_bins():
        loads[1].wait()
        tile = jnp.concatenate(
            [braw[pl.ds(h, 512, stride=2), :].astype(f32).astype(bf16) for h in range(2)], axis=1
        )
        source = lax.broadcasted_iota(jnp.int32, (BLOCK, BLOCK), 0)
        column = lax.broadcasted_iota(jnp.int32, (BLOCK, BLOCK), 1)
        wanted = ((column // 32) % 4) * 64 + (column // 128) * 32 + column % 32
        order = (source == wanted).astype(bf16)
        same = (source == column).astype(bf16)
        by_row = jnp.dot(tile, order, preferred_element_type=f32).astype(bf16)
        for lo in range(2):
            brow[lo] = by_row[:, lo * 128:(lo + 1) * 128].reshape(2, RING, 64, 128)
        by_col = lax.dot_general(same, tile, (((1,), (1,)), ((), ())),
                                 preferred_element_type=f32).astype(bf16)
        for hi in range(2):
            bcol[hi] = by_col[:, hi * BLOCK:(hi + 1) * BLOCK].reshape(RING, 2, STAT, BLOCK)

    def send_bins():
        for turn in range(2):
            to_x = x if turn == 0 else flip
            to_lo = lax.rem(to_x, 2)
            for dz in range(RING):
                to_z = wrap(z + dz)
                src, dst = brow.at[to_lo, :, to_z], d1buf.at[c, z, :, x_lo]
                if turn == 0 and dz == 0:
                    pltpu.make_async_copy(src, dst, d_recv.at[0]).start()
                else:
                    start(src, dst, bin_send.at[0], d_recv.at[0], device(to_x, y, to_z, c))
        for turn in range(2):
            to_hi = x_hi if turn == 0 else 1 - x_hi
            for dy in range(RING):
                to_y = wrap(y + dy)
                src, dst = bcol.at[to_hi, to_y], d2buf.at[c, y, x_hi]
                if turn == 0 and dy == 0:
                    pltpu.make_async_copy(src, dst, d_recv.at[1]).start()
                else:
                    start(src, dst, bin_send.at[1], d_recv.at[1], device(to_hi * 2 + x_lo, to_y, z, c))

    def share_bins():
        await_bytes(d1buf.at[c], d_recv.at[0])
        start(d1buf.at[c], d1buf.at[c], bin_send.at[2], d_recv.at[2], device(x, y, z, other))
        await_bytes(d2buf.at[c], d_recv.at[1])
        start(d2buf.at[c], d2buf.at[c], bin_send.at[2], d_recv.at[3], device(x, y, z, other))

    def wait_bins():
        await_bytes(d1buf.at[other], d_recv.at[2])
        await_bytes(d2buf.at[other], d_recv.at[3])
        loads[2].wait()
        table[1] = table[0]

    def lookups(row, blocks=range(RING)):
        wide = jnp.concatenate([table[0], table[1]], axis=1).astype(f32)
        table_wide = wide
        names = []
        for t in range(STAGES):
            for part in range(2):
                line = table_line(table_wide, BANDS * part, t)
                names.append(jnp.broadcast_to(line, (64, 128)))
        rx = wrap(x + ROW_SHIFT[row])
        rhi, rlo = lax.div(rx, 2), lax.rem(rx, 2)
        pieces = [d1buf[k, zz, rhi, rlo].astype(f32) for zz in range(RING) for k in range(CORES)]
        for yy in blocks:
            mirrored = d2buf[:, yy, rhi, rlo].astype(f32).astype(jnp.int32).reshape(64, BLOCK)
            for side in range(2):
                direct = jnp.concatenate(
                    [pieces[4 * side + i][:, yy * STAT:(yy + 1) * STAT] for i in range(4)], axis=1
                ).astype(jnp.int32)
                mirror = mirrored[:, side * 128:(side + 1) * 128]
                for t in range(STAGES):
                    for part in range(2):
                        tab = names[2 * t + part]
                        one = jnp.take_along_axis(tab, direct, axis=1, mode="promise_in_bounds")
                        two = jnp.take_along_axis(tab, mirror, axis=1, mode="promise_in_bounds")
                        value = one + two if part == 0 else one - two
                        dbuf[t, part, row, :, pl.ds(yy * BLOCK + side * 128, 128)] = value

    def table_line(wide, base, t):
        return jnp.where(c == 0, wide[base + t:base + t + 1], wide[base + 2 + t:base + 3 + t])

    def corr(t, dy):
        yy = wrap(y + dy)
        base = pl.multiple_of(yy * BLOCK, BLOCK)
        right = ybuf[t, pl.ds(yy * 8, 8)].reshape(BLOCK, WIDTH)
        for part in range(2):
            left = lbuf[t, part].reshape(ROWS, WIDTH)
            got = lax.dot_general(left, right, (((1,), (1,)), ((), ())), preferred_element_type=f32)
            value = got.reshape(RING, 64, BLOCK) * scale - dbuf[t, part, :, :, pl.ds(base, BLOCK)]
            sbuf[t, :, part, :, pl.ds(base, BLOCK)] = value.astype(bf16)

    def adjoint(t, half):
        left = sbuf[t, 2 * half:2 * half + 2].reshape(ROWS, COLS)
        for j in range(2):
            real = ybuf[t, :, :, j * 256:(j + 1) * 256].reshape(COLS, 256)
            imag = ybuf[t, :, :, HALF + j * 256:HALF + (j + 1) * 256].reshape(COLS, 256)
            a = jnp.dot(left, real, preferred_element_type=f32).reshape(2, 2, 64, 256)
            b = jnp.dot(left, imag, preferred_element_type=f32).reshape(2, 2, 64, 256)
            re = (a[:, 0] - b[:, 1]).reshape(2, CORES, STAT, 256)
            im = (b[:, 0] + a[:, 1]).reshape(2, CORES, STAT, 256)
            for value, base in ((re, j * 256), (im, HALF + j * 256)):
                pbuf[t, 2 * half:2 * half + 2, :, :, base:base + 256] = value
                hbuf[t, 2 * half:2 * half + 2, :, :, base:base + 256] = value.astype(bf16)

    def sums_first(t):
        up, down = wrap(x + 1), wrap(x - 1)
        start(hbuf.at[t, OPP, 0], rs1.at[t, 0], rs_send.at[t], rs_recv.at[t, 0], device(up, y, z, c))
        start(hbuf.at[t, OPP, 1], rs1.at[t, 1], rs_send.at[t], rs_recv.at[t, 1], device(down, y, z, c))
        start(hbuf.at[t, PLUS, 1], fbuf.at[c, t, 0], rs_send.at[t], f_recv.at[c, t, 0], device(up, y, z, 1))

    def sums_second(t):
        down = wrap(x - 1)
        start(hbuf.at[t, MINUS, 0], fbuf.at[c, t, 1], rs_send.at[t], f_recv.at[c, t, 1], device(down, y, z, 0))
        start(pbuf.at[t, OWN, other], nbuf.at[t], own_send.at[t], n_recv.at[t], device(x, y, z, other))

    def sums_forward(t):
        await_bytes(rs1.at[t, 0], rs_recv.at[t, 0])
        gbuf[t, 0] = (rs1[t, 0].astype(f32) + pbuf[t, PLUS, 0]).astype(bf16)
        start(gbuf.at[t, 0], fbuf.at[c, t, 0], fin_send.at[t], f_recv.at[c, t, 0],
              device(wrap(x + 1), y, z, 0))
        await_bytes(rs1.at[t, 1], rs_recv.at[t, 1])
        gbuf[t, 1] = (rs1[t, 1].astype(f32) + pbuf[t, MINUS, 1]).astype(bf16)
        start(gbuf.at[t, 1], fbuf.at[c, t, 1], fin_send.at[t], f_recv.at[c, t, 1],
              device(wrap(x - 1), y, z, 1))

    def store(band, value):
        value = value * (1.0 / math.sqrt(COLS * RING))
        for part in range(2):
            for j in range(4):
                piece = value[:, part * HALF + j * 128:part * HALF + (j + 1) * 128]
                out_ref[pl.ds(band * 8 + j * 2 + part, STAT, stride=32), :] = piece

    def sums_last(t):
        await_bytes(nbuf.at[t], n_recv.at[t])
        for core, mine in ((other, nbuf.at[t]), (c, pbuf.at[t, OWN, c])):
            for i in range(2):
                await_bytes(fbuf.at[core, t, i], f_recv.at[core, t, i])
            store(2 * core + t, mine[...] + fbuf[core, t, 0].astype(f32) + fbuf[core, t, 1].astype(f32))

    def sends_done(t):
        await_bytes(ybuf.at[t, pl.ds(0, 13)], hop_send.at[t])
        await_bytes(ybuf.at[t, pl.ds(0, 12)], q_send.at[t])
        await_bytes(ybuf.at[t, pl.ds(0, 12)], half_send.at[t])

    hop_p(0)
    hop_q(0)
    hop_x(0)
    make_bins()
    send_bins()
    hop_p(1)
    hop_q(1)
    hop_x(1)
    p_step(0)
    q_near(0)
    x_step(0)
    own_units(0)
    q_step(0,0)
    p_step(1)
    x_step(1)
    own_units(1)
    p_last(0)
    x_last(0)
    share_bins()
    q_step(0,1)
    q_step(0,2)
    q_near(1)
    q_step(1,0)
    wait_bins()
    lookups(0)
    lookups(1)
    q_step(0,3)
    p_last(1)
    lookups(2)
    lookups(3)
    x_last(1)
    q_last(0,0,0)
    corr(0,0)
    q_last(0,0,2)
    corr(0,1)
    q_step(1,1)
    q_step(1,2)
    q_last(0,0,1)
    corr(0,-1)
    q_last(0, 0, 3)
    for i in range(4):
        q_last(0, 1, i)
    corr(0, 2)
    q_step(1, 3)
    adjoint(0, 0)
    sums_first(0)
    adjoint(0, 1)
    sums_second(0)
    q_last(1,0,0)
    corr(1,0)
    q_last(1,0,2)
    corr(1,1)
    q_last(1,0,1)
    corr(1,-1)
    sums_forward(0)
    sends_done(0)
    for i in range(2):
        await_bytes(ybuf.at[0, pl.ds(0, 7), pl.ds(0, 16)], bin_send.at[i])
    await_bytes(ybuf.at[0, pl.ds(0, 8)], bin_send.at[2])
    q_last(1, 0, 3)
    for i in range(4):
        q_last(1, 1, i)
    corr(1, 2)
    adjoint(1, 0)
    sums_first(1)
    adjoint(1, 1)
    sums_second(1)
    sums_last(0)
    sums_forward(1)
    sends_done(1)
    await_bytes(hbuf.at[0, pl.ds(0, 2)], rs_send.at[0])
    await_bytes(nbuf.at[0], own_send.at[0])
    await_bytes(gbuf.at[0], fin_send.at[0])
    sums_last(1)
    await_bytes(hbuf.at[1, pl.ds(0, 2)], rs_send.at[1])
    await_bytes(nbuf.at[1], own_send.at[1])
    await_bytes(gbuf.at[1], fin_send.at[1])


def exchange(spectra, bins, table):
    f32, bf16, i32 = jnp.float32, jnp.bfloat16, jnp.int32
    dma, vmem = pltpu.SemaphoreType.DMA, pltpu.VMEM
    return pl.pallas_call(
        kernel,
        out_shape=jax.ShapeDtypeStruct((STAT * 32, 128), f32),
        in_specs=[pl.BlockSpec(memory_space=pltpu.HBM)] * 3,
        out_specs=pl.BlockSpec(memory_space=pltpu.VMEM),
        scratch_shapes=[
            vmem((STAT * 32, 128), bf16),
            vmem((STAT * 32, 128), f32),
            vmem((BANDS, STAT, WIDTH), bf16),
            vmem((1024, 128), i32),
            vmem((2, 2 * BANDS, 64), bf16),
            vmem((2, 2, RING, 64, 128), bf16),
            vmem((2, RING, 2, STAT, BLOCK), bf16),
            vmem((STAGES, 32, STAT, WIDTH), bf16),
            vmem((STAGES, 2, RING, CORES, STAT, WIDTH), bf16),
            vmem((CORES, RING, 2, 2, 64, 128), bf16),
            vmem((CORES, RING, 2, 2, STAT, BLOCK), bf16),
            vmem((STAGES, 2, RING, 64, COLS), f32),
            vmem((STAGES, RING, 2, 64, COLS), bf16),
            vmem((STAGES, RING, CORES, STAT, WIDTH), f32),
            vmem((STAGES, RING, CORES, STAT, WIDTH), bf16),
            vmem((STAGES, 2, STAT, WIDTH), bf16),
            vmem((STAGES, 2, STAT, WIDTH), bf16),
            vmem((CORES, STAGES, 2, STAT, WIDTH), bf16),
            vmem((STAGES, STAT, WIDTH), f32),
            dma((3,)), dma((STAGES,)), dma((STAGES,)), dma((STAGES,)), dma((3,)), dma((STAGES,)),
            dma((STAGES,)), dma((STAGES,)), dma((STAGES,)), dma((STAGES, CORES, 3)), dma((STAGES, CORES, 4, 3)),
            dma((STAGES, CORES, 3)), dma((4,)), dma((STAGES, 2)), dma((CORES, STAGES, 2)), dma((STAGES,)),
        ],
        compiler_params=pltpu.CompilerParams(
            collective_id=0, has_side_effects=True, vmem_limit_bytes=48 * 1024 * 1024
        ),
    )(spectra, bins, table)


def per_device(records, ref_bin, ref_table):
    spectra = records.reshape(STAT, 2, 16, 128).transpose(0, 2, 1, 3).reshape(STAT * 32, 128)
    args = (spectra, ref_bin.reshape(1024, 128), ref_table.T)
    out = exchange(*(pltpu.with_memory_space_constraint(arg, pltpu.HBM) for arg in args))
    return out.reshape(STAT, 16, 2, 128).transpose(0, 2, 1, 3).reshape(STAT, 2, 2048)


def solution(mesh):
    in_specs = (P(("grp", "sub"), None, None), P("grp", None, "sub", None), P())
    out_specs = P(("grp", "sub"), None, None)
    return jax.shard_map(
        per_device, mesh=mesh, in_specs=in_specs, out_specs=out_specs, check_vma=False
    )
```

```python
import math

import jax
import jax.numpy as jnp
from jax import lax
from jax.experimental import pallas as pl
from jax.experimental.pallas import tpu as pltpu
from jax.sharding import PartitionSpec as P

RING = 4
CORES = 2
BANDS = 4
STAGES = 2
STAT = 32
WIDTH = 1024
HALF = 512
COLS = 1024
ROWS = 256
BLOCK = 256
MESH = pl.DeviceIdType.MESH
OPP, PLUS, MINUS, OWN = 0, 1, 2, 3
ROW_SHIFT = (2, 1, 3, 0)
DIRECT = (0, 1)


def wrap(value):
    return lax.rem(value + RING, RING)


def device(x, y, z, core):
    return (y * 2 + lax.rem(x, 2), lax.div(x, 2) * 8 + z * 2 + core)


def kernel(
    raw_x, raw_bins, raw_table, out_ref,
    xraw, xwide, xbuf, braw, table, brow, bcol,
    ybuf, lbuf, d1buf, d2buf, dbuf, sbuf, pbuf, hbuf, rs1, gbuf, fbuf, nbuf,
    in_sem, hop_send, q_send, half_send, bin_send, rs_send, fin_send, own_send,
    own_recv, p_recv, q_recv, x_recv, d_recv, rs_recv, f_recv, n_recv,
):
    grp = lax.axis_index("grp")
    sub = lax.axis_index("sub")
    y, x_lo = lax.div(grp, 2), lax.rem(grp, 2)
    x_hi, z, c = lax.div(sub, 8), lax.rem(lax.div(sub, 2), RING), lax.rem(sub, 2)
    x = x_hi * 2 + x_lo
    other = 1 - c
    flip = x + 1 - 2 * x_lo
    scale = 2.0 / math.sqrt(HALF)
    f32, bf16 = jnp.float32, jnp.bfloat16

    def flow(k, p, q):
        yy = wrap(y + (1 - k) * p + k * q)
        zz = wrap(z + k * p + (1 - k) * q)
        return yy, zz

    def slot(k, p, q):
        yy, zz = flow(k, p, q)
        return (yy * RING + zz) * CORES + k

    def start(src, dst, send, recv, target):
        pltpu.make_async_remote_copy(
            src_ref=src, dst_ref=dst, send_sem=send, recv_sem=recv,
            device_id=target, device_id_type=MESH,
        ).start()

    def await_bytes(ref, sem):
        pltpu.make_async_copy(ref, ref, sem).wait()

    loads = [
        pltpu.make_async_copy(raw_x, xraw, in_sem.at[0]),
        pltpu.make_async_copy(raw_bins, braw, in_sem.at[1]),
        pltpu.make_async_copy(raw_table, table.at[0], in_sem.at[2]),
    ]
    for load in loads:
        load.start()
    barrier = pltpu.get_barrier_semaphore()
    near = [(wrap(x + d), y, z) for d in (1, 3)]
    near += [(x, wrap(y + d), z) for d in (1, 3)]
    near += [(x, y, wrap(z + d)) for d in (1, 3)]
    far = [(wrap(x + 2), wrap(y + d), z) for d in range(RING)] + [(x, wrap(y + 2), z)]
    far += [(flip, y, wrap(z + d)) for d in (1, 2, 3)] + [(x, y, wrap(z + 2))]
    peers = [device(x, y, z, other)] + [device(*chip, c) for chip in near + far]
    peers += [device(*chip, other) for chip in near]
    for peer in peers:
        pl.semaphore_signal(barrier, inc=1, device_id=peer, device_id_type=MESH)

    loads[0].wait()
    xwide[...] = xraw[...].astype(f32)
    for band in range(BANDS):
        for part in range(2):
            for j in range(4):
                line = xwide[pl.ds((band * 4 + j) * 2 + part, STAT, stride=32), :]
                xbuf[band, :, part * HALF + j * 128:part * HALF + (j + 1) * 128] = line.astype(bf16)
    pl.semaphore_wait(barrier, len(peers))

    def hop_p(t):
        here = slot(c, 0, 0)
        for index, sign in ((0, 1), (1, -1)):
            yy, zz = flow(c, sign, 0)
            for core in range(CORES):
                start(xbuf.at[2 * core + t], ybuf.at[t, here], hop_send.at[t],
                      p_recv.at[t, c, index], device(x, yy, zz, core))

    def hop_q(t):
        here = slot(c, 0, 0)
        for index, sign in ((0, 1), (1, -1)):
            yy, zz = flow(c, 0, sign)
            for core in range(CORES):
                start(xbuf.at[2 * core + t], ybuf.at[t, here], hop_send.at[t],
                      q_recv.at[t, c, 0, index], device(x, yy, zz, core))

    def hop_x(t):
        start(xbuf.at[2 * other + t], ybuf.at[t, slot(c, 0, 0)], hop_send.at[t], own_recv.at[t],
              device(x, y, z, other))
        for sign, index, row in ((1, 0, MINUS), (-1, 1, PLUS)):
            for core in range(CORES):
                start(xbuf.at[2 * core + t], lbuf.at[t, 0, row, c], hop_send.at[t],
                      x_recv.at[t, c, index], device(wrap(x + sign), y, z, core))

    def own_units(t):
        mine = xbuf[2 * c + t]
        ybuf[t, slot(c, 0, 0)] = mine
        lbuf[t, 0, OWN, c] = mine
        here = slot(other, 0, 0)
        await_bytes(ybuf.at[t, here], own_recv.at[t])
        lbuf[t, 0, OWN, other] = ybuf[t, here]

    SHIFT = (0, -1, 1, 2)

    def q_out(t, k, p_index):
        here = slot(k, SHIFT[p_index], 0)
        for sign, index in ((1, 0), (-1, 1)):
            yy, zz = flow(k, 0, sign)
            start(ybuf.at[t, here], ybuf.at[t, here], q_send.at[t],
                  q_recv.at[t, k, p_index, index], device(x, yy, zz, c))

    def p_step(t):
        for sign, index in ((-1, 0), (1, 1)):
            for k in range(CORES):
                here = slot(k, sign, 0)
                await_bytes(ybuf.at[t, here], p_recv.at[t, k, index])
                yy, zz = flow(k, -sign, 0)
                part = pl.ds(16 * index, 16)
                start(ybuf.at[t, here, part], ybuf.at[t, here, part], half_send.at[t],
                      p_recv.at[t, k, 2], device(x, yy, zz, c))

    def q_near(t):
        for p_index in (1, 2):
            for k in range(CORES):
                q_out(t, k, p_index)

    def p_last(t):
        for k in range(CORES):
            here = slot(k, 2, 0)
            await_bytes(ybuf.at[t, here], p_recv.at[t, k, 2])
            q_out(t, k, 3)
            if t in DIRECT:
                yy, zz = flow(k, 0, 2)
                start(ybuf.at[t, here], ybuf.at[t, here], q_send.at[t], q_recv.at[t, k, 3, 2],
                      device(x, yy, zz, c))

    def x_step(t):
        for row, index, sign in ((MINUS, 0, 1), (PLUS, 1, -1)):
            for k in range(CORES):
                await_bytes(lbuf.at[t, 0, row, k], x_recv.at[t, k, index])
                part = pl.ds(16 * index, 16)
                start(lbuf.at[t, 0, row, k, part], lbuf.at[t, 0, OPP, k, part], half_send.at[t],
                      x_recv.at[t, k, 2], device(wrap(x + sign), y, z, c))

    def x_last(t):
        for k in range(CORES):
            await_bytes(lbuf.at[t, 0, OPP, k], x_recv.at[t, k, 2])
        for row in range(RING):
            for k in range(CORES):
                lbuf[t, 1, row, k, :, :HALF] = lbuf[t, 0, row, k, :, HALF:]
                lbuf[t, 1, row, k, :, HALF:] = -lbuf[t, 0, row, k, :, :HALF]

    def q_step(t, p_index):
        p = SHIFT[p_index]
        for sign, index in ((-1, 0), (1, 1)):
            for k in range(CORES):
                here = slot(k, p, sign)
                await_bytes(ybuf.at[t, here], q_recv.at[t, k, p_index, index])
                if p_index == 3 and t in DIRECT:
                    continue
                yy, zz = flow(k, 0, -sign)
                part = pl.ds(16 * index, 16)
                start(ybuf.at[t, here, part], ybuf.at[t, here, part], half_send.at[t],
                      q_recv.at[t, k, p_index, 2], device(x, yy, zz, c))

    def q_last(t, k, p_index):
        await_bytes(ybuf.at[t, slot(k, SHIFT[p_index], 2)], q_recv.at[t, k, p_index, 2])

    def make_bins():
        loads[1].wait()
        tile = jnp.concatenate(
            [braw[pl.ds(h, 512, stride=2), :].astype(f32).astype(bf16) for h in range(2)], axis=1
        )
        source = lax.broadcasted_iota(jnp.int32, (BLOCK, BLOCK), 0)
        column = lax.broadcasted_iota(jnp.int32, (BLOCK, BLOCK), 1)
        wanted = ((column // 32) % 4) * 64 + (column // 128) * 32 + column % 32
        order = (source == wanted).astype(bf16)
        same = (source == column).astype(bf16)
        by_row = jnp.dot(tile, order, preferred_element_type=f32).astype(bf16)
        for lo in range(2):
            brow[lo] = by_row[:, lo * 128:(lo + 1) * 128].reshape(2, RING, 64, 128)
        by_col = lax.dot_general(same, tile, (((1,), (1,)), ((), ())),
                                 preferred_element_type=f32).astype(bf16)
        for hi in range(2):
            bcol[hi] = by_col[:, hi * BLOCK:(hi + 1) * BLOCK].reshape(RING, 2, STAT, BLOCK)

    def send_bins():
        for turn in range(2):
            to_x = x if turn == 0 else flip
            to_lo = lax.rem(to_x, 2)
            for dz in range(RING):
                to_z = wrap(z + dz)
                src, dst = brow.at[to_lo, :, to_z], d1buf.at[c, z, :, x_lo]
                if turn == 0 and dz == 0:
                    pltpu.make_async_copy(src, dst, d_recv.at[0]).start()
                else:
                    start(src, dst, bin_send.at[0], d_recv.at[0], device(to_x, y, to_z, c))
        for turn in range(2):
            to_hi = x_hi if turn == 0 else 1 - x_hi
            for dy in range(RING):
                to_y = wrap(y + dy)
                src, dst = bcol.at[to_hi, to_y], d2buf.at[c, y, x_hi]
                if turn == 0 and dy == 0:
                    pltpu.make_async_copy(src, dst, d_recv.at[1]).start()
                else:
                    start(src, dst, bin_send.at[1], d_recv.at[1], device(to_hi * 2 + x_lo, to_y, z, c))

    def share_bins():
        await_bytes(d1buf.at[c], d_recv.at[0])
        start(d1buf.at[c], d1buf.at[c], bin_send.at[2], d_recv.at[2], device(x, y, z, other))
        await_bytes(d2buf.at[c], d_recv.at[1])
        start(d2buf.at[c], d2buf.at[c], bin_send.at[2], d_recv.at[3], device(x, y, z, other))

    def wait_bins():
        await_bytes(d1buf.at[other], d_recv.at[2])
        await_bytes(d2buf.at[other], d_recv.at[3])
        loads[2].wait()
        table[1] = table[0]

    def lookups(row, blocks=range(RING)):
        wide = jnp.concatenate([table[0], table[1]], axis=1).astype(f32)
        table_wide = wide
        names = []
        for t in range(STAGES):
            for part in range(2):
                line = table_line(table_wide, BANDS * part, t)
                names.append(jnp.broadcast_to(line, (64, 128)))
        rx = wrap(x + ROW_SHIFT[row])
        rhi, rlo = lax.div(rx, 2), lax.rem(rx, 2)
        pieces = [d1buf[k, zz, rhi, rlo].astype(f32) for zz in range(RING) for k in range(CORES)]
        for yy in blocks:
            mirrored = d2buf[:, yy, rhi, rlo].astype(f32).astype(jnp.int32).reshape(64, BLOCK)
            for side in range(2):
                direct = jnp.concatenate(
                    [pieces[4 * side + i][:, yy * STAT:(yy + 1) * STAT] for i in range(4)], axis=1
                ).astype(jnp.int32)
                mirror = mirrored[:, side * 128:(side + 1) * 128]
                for t in range(STAGES):
                    for part in range(2):
                        tab = names[2 * t + part]
                        one = jnp.take_along_axis(tab, direct, axis=1, mode="promise_in_bounds")
                        two = jnp.take_along_axis(tab, mirror, axis=1, mode="promise_in_bounds")
                        value = one + two if part == 0 else one - two
                        dbuf[t, part, row, :, pl.ds(yy * BLOCK + side * 128, 128)] = value

    def table_line(wide, base, t):
        return jnp.where(c == 0, wide[base + t:base + t + 1], wide[base + 2 + t:base + 3 + t])

    def corr(t, dy):
        yy = wrap(y + dy)
        base = pl.multiple_of(yy * BLOCK, BLOCK)
        right = ybuf[t, pl.ds(yy * 8, 8)].reshape(BLOCK, WIDTH)
        for part in range(2):
            left = lbuf[t, part].reshape(ROWS, WIDTH)
            got = lax.dot_general(left, right, (((1,), (1,)), ((), ())), preferred_element_type=f32)
            value = got.reshape(RING, 64, BLOCK) * scale - dbuf[t, part, :, :, pl.ds(base, BLOCK)]
            sbuf[t, :, part, :, pl.ds(base, BLOCK)] = value.astype(bf16)

    def adjoint(t, half, j):
        rows = slice(2 * half, 2 * half + 2)
        left = sbuf[t, rows].reshape(ROWS, COLS)
        real = ybuf[t, :, :, j * 256:(j + 1) * 256].reshape(COLS, 256)
        imag = ybuf[t, :, :, HALF + j * 256:HALF + (j + 1) * 256].reshape(COLS, 256)
        a = jnp.dot(left, real, preferred_element_type=f32).reshape(2, 2, 64, 256)
        b = jnp.dot(left, imag, preferred_element_type=f32).reshape(2, 2, 64, 256)
        re = (a[:, 0] - b[:, 1]).reshape(2, CORES, STAT, 256)
        im = (b[:, 0] + a[:, 1]).reshape(2, CORES, STAT, 256)
        for value, cols in ((re, slice(0, 256)), (im, slice(256, HALF))):
            pbuf[t, rows, :, j, :, cols] = value
            hbuf[t, rows, :, j, :, cols] = value.astype(bf16)

    def sums_first(t, j):
        for k, to in ((0, wrap(x + 1)), (1, wrap(x - 1))):
            start(hbuf.at[t, OPP, k, j], rs1.at[t, k, j], rs_send.at[t], rs_recv.at[t, k, j],
                  device(to, y, z, c))

    def sums_second(t):
        up, down = wrap(x + 1), wrap(x - 1)
        start(hbuf.at[t, PLUS, 1], fbuf.at[c, t, 0], rs_send.at[t], f_recv.at[c, t, 0], device(up, y, z, 1))
        start(hbuf.at[t, MINUS, 0], fbuf.at[c, t, 1], rs_send.at[t], f_recv.at[c, t, 1], device(down, y, z, 0))
        start(pbuf.at[t, OWN, other], nbuf.at[t], own_send.at[t], n_recv.at[t], device(x, y, z, other))

    def sums_forward(t):
        for j in range(2):
            for k, row, to in ((0, PLUS, wrap(x + 1)), (1, MINUS, wrap(x - 1))):
                await_bytes(rs1.at[t, k, j], rs_recv.at[t, k, j])
                gbuf[t, k, j] = (rs1[t, k, j].astype(f32) + pbuf[t, row, k, j]).astype(bf16)
                start(gbuf.at[t, k, j], fbuf.at[c, t, k, j], fin_send.at[t], f_recv.at[c, t, k],
                      device(to, y, z, k))

    def store(band, value):
        value = value * (1.0 / math.sqrt(COLS * RING))
        for part in range(2):
            for j in range(4):
                at = part * 256 + (j % 2) * 128
                piece = value[j // 2, :, at:at + 128]
                out_ref[pl.ds(band * 8 + j * 2 + part, STAT, stride=32), :] = piece

    def sums_last(t):
        await_bytes(nbuf.at[t], n_recv.at[t])
        for core, mine in ((other, nbuf.at[t]), (c, pbuf.at[t, OWN, c])):
            for i in range(2):
                await_bytes(fbuf.at[core, t, i], f_recv.at[core, t, i])
            store(2 * core + t, mine[...] + fbuf[core, t, 0].astype(f32) + fbuf[core, t, 1].astype(f32))

    def sends_done(t):
        await_bytes(ybuf.at[t, pl.ds(0, 13)], hop_send.at[t])
        straight = 2 if t in DIRECT else 0
        await_bytes(ybuf.at[t, pl.ds(0, 12 + straight)], q_send.at[t])
        await_bytes(ybuf.at[t, pl.ds(0, 12 - straight)], half_send.at[t])

    hop_p(0)
    hop_q(0)
    hop_x(0)
    make_bins()
    send_bins()
    hop_p(1)
    hop_q(1)
    hop_x(1)
    p_step(0)
    q_near(0)
    x_step(0)
    own_units(0)
    q_step(0,0)
    p_step(1)
    x_step(1)
    own_units(1)
    p_last(0)
    x_last(0)
    share_bins()
    q_step(0,1)
    q_step(0,2)
    q_near(1)
    q_step(1,0)
    wait_bins()
    lookups(0, range(0, 2))
    lookups(0, range(2, 4))
    lookups(1, range(0, 2))
    q_step(0,3)
    lookups(1, range(2, 4))
    p_last(1)
    lookups(2, range(0, 2))
    lookups(2, range(2, 4))
    x_last(1)
    q_step(1,1)
    lookups(3, range(0, 2))
    lookups(3, range(2, 4))
    q_step(1,2)
    q_last(0,0,0)
    corr(0,0)
    q_last(0,0,2)
    corr(0,1)
    q_last(0,0,1)
    corr(0,-1)
    q_last(0, 0, 3)
    for i in range(4):
        q_last(0, 1, i)
    corr(0, 2)
    adjoint(0, 0, 0)
    sums_first(0, 0)
    adjoint(0, 0, 1)
    sums_first(0, 1)
    adjoint(0, 1, 0)
    adjoint(0, 1, 1)
    sums_second(0)
    q_last(1,0,0)
    corr(1,0)
    q_step(1, 3)
    q_last(1,0,2)
    corr(1,1)
    q_last(1,0,1)
    corr(1,-1)
    sums_forward(0)
    sends_done(0)
    for i in range(2):
        await_bytes(ybuf.at[0, pl.ds(0, 7), pl.ds(0, 16)], bin_send.at[i])
    await_bytes(ybuf.at[0, pl.ds(0, 8)], bin_send.at[2])
    q_last(1, 0, 3)
    for i in range(4):
        q_last(1, 1, i)
    corr(1, 2)
    adjoint(1, 0, 0)
    sums_first(1, 0)
    adjoint(1, 0, 1)
    sums_first(1, 1)
    adjoint(1, 1, 0)
    adjoint(1, 1, 1)
    sums_second(1)
    sums_last(0)
    sums_forward(1)
    sends_done(1)
    await_bytes(hbuf.at[0, pl.ds(0, 2)], rs_send.at[0])
    await_bytes(nbuf.at[0], own_send.at[0])
    await_bytes(gbuf.at[0], fin_send.at[0])
    sums_last(1)
    await_bytes(hbuf.at[1, pl.ds(0, 2)], rs_send.at[1])
    await_bytes(nbuf.at[1], own_send.at[1])
    await_bytes(gbuf.at[1], fin_send.at[1])


def exchange(spectra, bins, table):
    f32, bf16, i32 = jnp.float32, jnp.bfloat16, jnp.int32
    dma, vmem = pltpu.SemaphoreType.DMA, pltpu.VMEM
    return pl.pallas_call(
        kernel,
        out_shape=jax.ShapeDtypeStruct((STAT * 32, 128), f32),
        in_specs=[pl.BlockSpec(memory_space=pltpu.HBM)] * 3,
        out_specs=pl.BlockSpec(memory_space=pltpu.VMEM),
        scratch_shapes=[
            vmem((STAT * 32, 128), bf16),
            vmem((STAT * 32, 128), f32),
            vmem((BANDS, STAT, WIDTH), bf16),
            vmem((1024, 128), i32),
            vmem((2, 2 * BANDS, 64), bf16),
            vmem((2, 2, RING, 64, 128), bf16),
            vmem((2, RING, 2, STAT, BLOCK), bf16),
            vmem((STAGES, 32, STAT, WIDTH), bf16),
            vmem((STAGES, 2, RING, CORES, STAT, WIDTH), bf16),
            vmem((CORES, RING, 2, 2, 64, 128), bf16),
            vmem((CORES, RING, 2, 2, STAT, BLOCK), bf16),
            vmem((STAGES, 2, RING, 64, COLS), f32),
            vmem((STAGES, RING, 2, 64, COLS), bf16),
            vmem((STAGES, RING, CORES, 2, STAT, HALF), f32),
            vmem((STAGES, RING, CORES, 2, STAT, HALF), bf16),
            vmem((STAGES, 2, 2, STAT, HALF), bf16),
            vmem((STAGES, 2, 2, STAT, HALF), bf16),
            vmem((CORES, STAGES, 2, 2, STAT, HALF), bf16),
            vmem((STAGES, 2, STAT, HALF), f32),
            dma((3,)), dma((STAGES,)), dma((STAGES,)), dma((STAGES,)), dma((3,)), dma((STAGES,)),
            dma((STAGES,)), dma((STAGES,)), dma((STAGES,)), dma((STAGES, CORES, 3)), dma((STAGES, CORES, 4, 3)),
            dma((STAGES, CORES, 3)), dma((4,)), dma((STAGES, 2, 2)), dma((CORES, STAGES, 2)), dma((STAGES,)),
        ],
        compiler_params=pltpu.CompilerParams(
            collective_id=0, has_side_effects=True, vmem_limit_bytes=48 * 1024 * 1024
        ),
    )(spectra, bins, table)


def per_device(records, ref_bin, ref_table):
    spectra = records.reshape(STAT, 2, 16, 128).transpose(0, 2, 1, 3).reshape(STAT * 32, 128)
    args = (spectra, ref_bin.reshape(1024, 128), ref_table.T)
    out = exchange(*(pltpu.with_memory_space_constraint(arg, pltpu.HBM) for arg in args))
    return out.reshape(STAT, 16, 2, 128).transpose(0, 2, 1, 3).reshape(STAT, 2, 2048)


def solution(mesh):
    in_specs = (P(("grp", "sub"), None, None), P("grp", None, "sub", None), P())
    out_specs = P(("grp", "sub"), None, None)
    return jax.shard_map(
        per_device, mesh=mesh, in_specs=in_specs, out_specs=out_specs, check_vma=False
    )
```

```python
import math

import jax
import jax.numpy as jnp
from jax import lax
from jax.experimental import pallas as pl
from jax.experimental.pallas import tpu as pltpu
from jax.sharding import PartitionSpec as P

RING = 4
CORES = 2
BANDS = 4
STAGES = 2
STAT = 32
WIDTH = 1024
HALF = 512
COLS = 1024
ROWS = 256
BLOCK = 256
MESH = pl.DeviceIdType.MESH
OPP, PLUS, MINUS, OWN = 0, 1, 2, 3
ROW_SHIFT = (2, 1, 3, 0)
DIRECT = (0, 1)


def wrap(value):
    return lax.rem(value + RING, RING)


def device(x, y, z, core):
    return (y * 2 + lax.rem(x, 2), lax.div(x, 2) * 8 + z * 2 + core)


def kernel(
    raw_x, raw_bins, raw_table, out_ref,
    xraw, xwide, xbuf, braw, table, brow, bcol,
    ybuf, lbuf, d1buf, d2buf, dbuf, sbuf, pbuf, hbuf, rs1, gbuf, fbuf, nbuf,
    in_sem, hop_send, q_send, half_send, bin_send, rs_send, fin_send, own_send,
    own_recv, p_recv, q_recv, x_recv, d_recv, rs_recv, f_recv, n_recv,
):
    grp = lax.axis_index("grp")
    sub = lax.axis_index("sub")
    y, x_lo = lax.div(grp, 2), lax.rem(grp, 2)
    x_hi, z, c = lax.div(sub, 8), lax.rem(lax.div(sub, 2), RING), lax.rem(sub, 2)
    x = x_hi * 2 + x_lo
    other = 1 - c
    flip = x + 1 - 2 * x_lo
    scale = 2.0 / math.sqrt(HALF)
    f32, bf16 = jnp.float32, jnp.bfloat16

    def flow(k, p, q):
        yy = wrap(y + (1 - k) * p + k * q)
        zz = wrap(z + k * p + (1 - k) * q)
        return yy, zz

    def slot(k, p, q):
        yy, zz = flow(k, p, q)
        return (yy * RING + zz) * CORES + k

    def start(src, dst, send, recv, target):
        pltpu.make_async_remote_copy(
            src_ref=src, dst_ref=dst, send_sem=send, recv_sem=recv,
            device_id=target, device_id_type=MESH,
        ).start()

    def await_bytes(ref, sem):
        pltpu.make_async_copy(ref, ref, sem).wait()

    loads = [
        pltpu.make_async_copy(raw_x, xraw, in_sem.at[0]),
        pltpu.make_async_copy(raw_bins, braw, in_sem.at[1]),
        pltpu.make_async_copy(raw_table, table.at[0], in_sem.at[2]),
    ]
    for load in loads:
        load.start()
    barrier = pltpu.get_barrier_semaphore()
    near = [(wrap(x + d), y, z) for d in (1, 3)]
    near += [(x, wrap(y + d), z) for d in (1, 3)]
    near += [(x, y, wrap(z + d)) for d in (1, 3)]
    far = [(wrap(x + 2), wrap(y + d), z) for d in range(RING)] + [(x, wrap(y + 2), z)]
    far += [(flip, y, wrap(z + d)) for d in (1, 2, 3)] + [(x, y, wrap(z + 2))]
    peers = [device(x, y, z, other)] + [device(*chip, c) for chip in near + far]
    peers += [device(*chip, other) for chip in near]
    for peer in peers:
        pl.semaphore_signal(barrier, inc=1, device_id=peer, device_id_type=MESH)

    loads[0].wait()
    xwide[...] = xraw[...].astype(f32)
    for band in range(BANDS):
        for part in range(2):
            for j in range(4):
                line = xwide[pl.ds((band * 4 + j) * 2 + part, STAT, stride=32), :]
                xbuf[band, :, part * HALF + j * 128:part * HALF + (j + 1) * 128] = line.astype(bf16)
    pl.semaphore_wait(barrier, len(peers))

    def hop_p(t):
        here = slot(c, 0, 0)
        for index, sign in ((0, 1), (1, -1)):
            yy, zz = flow(c, sign, 0)
            for core in range(CORES):
                start(xbuf.at[2 * core + t], ybuf.at[t, here], hop_send.at[t],
                      p_recv.at[t, c, index], device(x, yy, zz, core))

    def hop_q(t):
        here = slot(c, 0, 0)
        for index, sign in ((0, 1), (1, -1)):
            yy, zz = flow(c, 0, sign)
            for core in range(CORES):
                start(xbuf.at[2 * core + t], ybuf.at[t, here], hop_send.at[t],
                      q_recv.at[t, c, 0, index], device(x, yy, zz, core))

    def hop_x(t):
        start(xbuf.at[2 * other + t], ybuf.at[t, slot(c, 0, 0)], hop_send.at[t], own_recv.at[t],
              device(x, y, z, other))
        for sign, index, row in ((1, 0, MINUS), (-1, 1, PLUS)):
            for core in range(CORES):
                start(xbuf.at[2 * core + t], lbuf.at[t, 0, row, c], hop_send.at[t],
                      x_recv.at[t, c, index], device(wrap(x + sign), y, z, core))

    def own_units(t):
        mine = xbuf[2 * c + t]
        ybuf[t, slot(c, 0, 0)] = mine
        lbuf[t, 0, OWN, c] = mine
        here = slot(other, 0, 0)
        await_bytes(ybuf.at[t, here], own_recv.at[t])
        lbuf[t, 0, OWN, other] = ybuf[t, here]

    SHIFT = (0, -1, 1, 2)

    def q_out(t, k, p_index):
        here = slot(k, SHIFT[p_index], 0)
        for sign, index in ((1, 0), (-1, 1)):
            yy, zz = flow(k, 0, sign)
            start(ybuf.at[t, here], ybuf.at[t, here], q_send.at[t],
                  q_recv.at[t, k, p_index, index], device(x, yy, zz, c))

    def p_step(t):
        for sign, index in ((-1, 0), (1, 1)):
            for k in range(CORES):
                here = slot(k, sign, 0)
                await_bytes(ybuf.at[t, here], p_recv.at[t, k, index])
                yy, zz = flow(k, -sign, 0)
                part = pl.ds(16 * index, 16)
                start(ybuf.at[t, here, part], ybuf.at[t, here, part], half_send.at[t],
                      p_recv.at[t, k, 2], device(x, yy, zz, c))

    def q_near(t):
        for p_index in (1, 2):
            for k in range(CORES):
                q_out(t, k, p_index)

    def p_last(t):
        for k in range(CORES):
            here = slot(k, 2, 0)
            await_bytes(ybuf.at[t, here], p_recv.at[t, k, 2])
            q_out(t, k, 3)
            if t in DIRECT:
                yy, zz = flow(k, 0, 2)
                start(ybuf.at[t, here], ybuf.at[t, here], q_send.at[t], q_recv.at[t, k, 3, 2],
                      device(x, yy, zz, c))

    def x_step(t):
        for row, index, sign in ((MINUS, 0, 1), (PLUS, 1, -1)):
            for k in range(CORES):
                await_bytes(lbuf.at[t, 0, row, k], x_recv.at[t, k, index])
                part = pl.ds(16 * index, 16)
                start(lbuf.at[t, 0, row, k, part], lbuf.at[t, 0, OPP, k, part], half_send.at[t],
                      x_recv.at[t, k, 2], device(wrap(x + sign), y, z, c))

    def x_last(t):
        for k in range(CORES):
            await_bytes(lbuf.at[t, 0, OPP, k], x_recv.at[t, k, 2])
        for row in range(RING):
            for k in range(CORES):
                lbuf[t, 1, row, k, :, :HALF] = lbuf[t, 0, row, k, :, HALF:]
                lbuf[t, 1, row, k, :, HALF:] = -lbuf[t, 0, row, k, :, :HALF]

    def q_step(t, p_index):
        p = SHIFT[p_index]
        for sign, index in ((-1, 0), (1, 1)):
            for k in range(CORES):
                here = slot(k, p, sign)
                await_bytes(ybuf.at[t, here], q_recv.at[t, k, p_index, index])
                if p_index == 3 and t in DIRECT:
                    continue
                yy, zz = flow(k, 0, -sign)
                part = pl.ds(16 * index, 16)
                start(ybuf.at[t, here, part], ybuf.at[t, here, part], half_send.at[t],
                      q_recv.at[t, k, p_index, 2], device(x, yy, zz, c))

    def q_last(t, k, p_index):
        await_bytes(ybuf.at[t, slot(k, SHIFT[p_index], 2)], q_recv.at[t, k, p_index, 2])

    def make_bins():
        loads[1].wait()
        tile = jnp.concatenate(
            [braw[pl.ds(h, 512, stride=2), :].astype(f32).astype(bf16) for h in range(2)], axis=1
        )
        source = lax.broadcasted_iota(jnp.int32, (BLOCK, BLOCK), 0)
        column = lax.broadcasted_iota(jnp.int32, (BLOCK, BLOCK), 1)
        wanted = ((column // 32) % 4) * 64 + (column // 128) * 32 + column % 32
        order = (source == wanted).astype(bf16)
        same = (source == column).astype(bf16)
        by_row = jnp.dot(tile, order, preferred_element_type=f32).astype(bf16)
        for lo in range(2):
            brow[lo] = by_row[:, lo * 128:(lo + 1) * 128].reshape(2, RING, 64, 128)
        by_col = lax.dot_general(same, tile, (((1,), (1,)), ((), ())),
                                 preferred_element_type=f32).astype(bf16)
        for hi in range(2):
            bcol[hi] = by_col[:, hi * BLOCK:(hi + 1) * BLOCK].reshape(RING, 2, STAT, BLOCK)

    def send_bins():
        for turn in range(2):
            to_x = x if turn == 0 else flip
            to_lo = lax.rem(to_x, 2)
            for dz in range(RING):
                to_z = wrap(z + dz)
                src, dst = brow.at[to_lo, :, to_z], d1buf.at[c, z, :, x_lo]
                if turn == 0 and dz == 0:
                    pltpu.make_async_copy(src, dst, d_recv.at[0]).start()
                else:
                    start(src, dst, bin_send.at[0], d_recv.at[0], device(to_x, y, to_z, c))
        for turn in range(2):
            to_hi = x_hi if turn == 0 else 1 - x_hi
            for dy in range(RING):
                to_y = wrap(y + dy)
                src, dst = bcol.at[to_hi, to_y], d2buf.at[c, y, x_hi]
                if turn == 0 and dy == 0:
                    pltpu.make_async_copy(src, dst, d_recv.at[1]).start()
                else:
                    start(src, dst, bin_send.at[1], d_recv.at[1], device(to_hi * 2 + x_lo, to_y, z, c))

    def share_bins():
        await_bytes(d1buf.at[c], d_recv.at[0])
        start(d1buf.at[c], d1buf.at[c], bin_send.at[2], d_recv.at[2], device(x, y, z, other))
        await_bytes(d2buf.at[c], d_recv.at[1])
        start(d2buf.at[c], d2buf.at[c], bin_send.at[2], d_recv.at[3], device(x, y, z, other))

    def wait_bins():
        await_bytes(d1buf.at[other], d_recv.at[2])
        await_bytes(d2buf.at[other], d_recv.at[3])
        loads[2].wait()
        table[1] = table[0]

    def lookups(row, blocks=range(RING)):
        wide = jnp.concatenate([table[0], table[1]], axis=1).astype(f32)
        table_wide = wide
        names = []
        for t in range(STAGES):
            for part in range(2):
                line = table_line(table_wide, BANDS * part, t)
                names.append(jnp.broadcast_to(line, (64, 128)))
        rx = wrap(x + ROW_SHIFT[row])
        rhi, rlo = lax.div(rx, 2), lax.rem(rx, 2)
        pieces = [d1buf[k, zz, rhi, rlo].astype(f32) for zz in range(RING) for k in range(CORES)]
        for yy in blocks:
            mirrored = d2buf[:, yy, rhi, rlo].astype(f32).astype(jnp.int32).reshape(64, BLOCK)
            for side in range(2):
                direct = jnp.concatenate(
                    [pieces[4 * side + i][:, yy * STAT:(yy + 1) * STAT] for i in range(4)], axis=1
                ).astype(jnp.int32)
                mirror = mirrored[:, side * 128:(side + 1) * 128]
                for t in range(STAGES):
                    for part in range(2):
                        tab = names[2 * t + part]
                        one = jnp.take_along_axis(tab, direct, axis=1, mode="promise_in_bounds")
                        two = jnp.take_along_axis(tab, mirror, axis=1, mode="promise_in_bounds")
                        value = one + two if part == 0 else one - two
                        dbuf[t, part, row, :, pl.ds(yy * BLOCK + side * 128, 128)] = value

    def table_line(wide, base, t):
        return jnp.where(c == 0, wide[base + t:base + t + 1], wide[base + 2 + t:base + 3 + t])

    def corr(t, dy):
        yy = wrap(y + dy)
        base = pl.multiple_of(yy * BLOCK, BLOCK)
        right = ybuf[t, pl.ds(yy * 8, 8)].reshape(BLOCK, WIDTH)
        for part in range(2):
            left = lbuf[t, part].reshape(ROWS, WIDTH)
            got = lax.dot_general(left, right, (((1,), (1,)), ((), ())), preferred_element_type=f32)
            value = got.reshape(RING, 64, BLOCK) * scale - dbuf[t, part, :, :, pl.ds(base, BLOCK)]
            sbuf[t, :, part, :, pl.ds(base, BLOCK)] = value.astype(bf16)

    def adjoint(t, half, j):
        rows = slice(2 * half, 2 * half + 2)
        left = sbuf[t, rows].reshape(ROWS, COLS)
        real = ybuf[t, :, :, j * 256:(j + 1) * 256].reshape(COLS, 256)
        imag = ybuf[t, :, :, HALF + j * 256:HALF + (j + 1) * 256].reshape(COLS, 256)
        a = jnp.dot(left, real, preferred_element_type=f32).reshape(2, 2, 64, 256)
        b = jnp.dot(left, imag, preferred_element_type=f32).reshape(2, 2, 64, 256)
        re = (a[:, 0] - b[:, 1]).reshape(2, CORES, STAT, 256)
        im = (b[:, 0] + a[:, 1]).reshape(2, CORES, STAT, 256)
        for value, cols in ((re, slice(0, 256)), (im, slice(256, HALF))):
            pbuf[t, rows, :, j, :, cols] = value
            hbuf[t, rows, :, j, :, cols] = value.astype(bf16)

    def sums_first(t, j):
        for k, to in ((0, wrap(x + 1)), (1, wrap(x - 1))):
            start(hbuf.at[t, OPP, k, j], rs1.at[t, k, j], rs_send.at[t], rs_recv.at[t, k, j],
                  device(to, y, z, c))

    def sums_second(t):
        up, down = wrap(x + 1), wrap(x - 1)
        start(hbuf.at[t, PLUS, 1], fbuf.at[c, t, 0], rs_send.at[t], f_recv.at[c, t, 0], device(up, y, z, 1))
        start(hbuf.at[t, MINUS, 0], fbuf.at[c, t, 1], rs_send.at[t], f_recv.at[c, t, 1], device(down, y, z, 0))
        start(pbuf.at[t, OWN, other], nbuf.at[t], own_send.at[t], n_recv.at[t], device(x, y, z, other))

    def sums_forward(t):
        for j in range(2):
            for k, row, to in ((0, PLUS, wrap(x + 1)), (1, MINUS, wrap(x - 1))):
                await_bytes(rs1.at[t, k, j], rs_recv.at[t, k, j])
                gbuf[t, k, j] = (rs1[t, k, j].astype(f32) + pbuf[t, row, k, j]).astype(bf16)
                start(gbuf.at[t, k, j], fbuf.at[c, t, k, j], fin_send.at[t], f_recv.at[c, t, k],
                      device(to, y, z, k))

    def store(band, value):
        value = value * (1.0 / math.sqrt(COLS * RING))
        for part in range(2):
            for j in range(4):
                at = part * 256 + (j % 2) * 128
                piece = value[j // 2, :, at:at + 128]
                out_ref[pl.ds(band * 8 + j * 2 + part, STAT, stride=32), :] = piece

    def sums_last(t):
        await_bytes(nbuf.at[t], n_recv.at[t])
        for core, mine in ((other, nbuf.at[t]), (c, pbuf.at[t, OWN, c])):
            for i in range(2):
                await_bytes(fbuf.at[core, t, i], f_recv.at[core, t, i])
            store(2 * core + t, mine[...] + fbuf[core, t, 0].astype(f32) + fbuf[core, t, 1].astype(f32))

    def sends_done(t):
        await_bytes(ybuf.at[t, pl.ds(0, 13)], hop_send.at[t])
        straight = 2 if t in DIRECT else 0
        await_bytes(ybuf.at[t, pl.ds(0, 12 + straight)], q_send.at[t])
        await_bytes(ybuf.at[t, pl.ds(0, 12 - straight)], half_send.at[t])

    hop_p(0)
    hop_q(0)
    hop_x(0)
    make_bins()
    send_bins()
    hop_p(1)
    hop_q(1)
    hop_x(1)
    p_step(0)
    q_near(0)
    x_step(0)
    own_units(0)
    q_step(0,0)
    p_step(1)
    x_step(1)
    own_units(1)
    p_last(0)
    x_last(0)
    share_bins()
    q_near(1)
    q_step(0,1)
    q_step(0,2)
    q_step(1,0)
    wait_bins()
    lookups(0, range(0, 2))
    lookups(0, range(2, 4))
    lookups(1, range(0, 2))
    q_step(0,3)
    lookups(1, range(2, 4))
    p_last(1)
    lookups(2, range(0, 2))
    lookups(2, range(2, 4))
    x_last(1)
    q_step(1,1)
    lookups(3, range(0, 2))
    lookups(3, range(2, 4))
    q_step(1,2)
    q_last(0,0,0)
    corr(0,0)
    q_last(0,0,2)
    corr(0,1)
    q_last(0,0,1)
    corr(0,-1)
    q_last(0, 0, 3)
    for i in range(4):
        q_last(0, 1, i)
    corr(0, 2)
    adjoint(0, 0, 0)
    sums_first(0, 0)
    adjoint(0, 0, 1)
    sums_first(0, 1)
    adjoint(0, 1, 0)
    adjoint(0, 1, 1)
    sums_second(0)
    q_last(1,0,0)
    corr(1,0)
    q_step(1, 3)
    q_last(1,0,2)
    corr(1,1)
    q_last(1,0,1)
    corr(1,-1)
    sums_forward(0)
    sends_done(0)
    for i in range(2):
        await_bytes(ybuf.at[0, pl.ds(0, 7), pl.ds(0, 16)], bin_send.at[i])
    await_bytes(ybuf.at[0, pl.ds(0, 8)], bin_send.at[2])
    q_last(1, 0, 3)
    for i in range(4):
        q_last(1, 1, i)
    corr(1, 2)
    adjoint(1, 0, 0)
    sums_first(1, 0)
    adjoint(1, 0, 1)
    sums_first(1, 1)
    adjoint(1, 1, 0)
    adjoint(1, 1, 1)
    sums_second(1)
    sums_last(0)
    sums_forward(1)
    sends_done(1)
    await_bytes(hbuf.at[0, pl.ds(0, 2)], rs_send.at[0])
    await_bytes(nbuf.at[0], own_send.at[0])
    await_bytes(gbuf.at[0], fin_send.at[0])
    sums_last(1)
    await_bytes(hbuf.at[1, pl.ds(0, 2)], rs_send.at[1])
    await_bytes(nbuf.at[1], own_send.at[1])
    await_bytes(gbuf.at[1], fin_send.at[1])


def exchange(spectra, bins, table):
    f32, bf16, i32 = jnp.float32, jnp.bfloat16, jnp.int32
    dma, vmem = pltpu.SemaphoreType.DMA, pltpu.VMEM
    return pl.pallas_call(
        kernel,
        out_shape=jax.ShapeDtypeStruct((STAT * 32, 128), f32),
        in_specs=[pl.BlockSpec(memory_space=pltpu.HBM)] * 3,
        out_specs=pl.BlockSpec(memory_space=pltpu.VMEM),
        scratch_shapes=[
            vmem((STAT * 32, 128), bf16),
            vmem((STAT * 32, 128), f32),
            vmem((BANDS, STAT, WIDTH), bf16),
            vmem((1024, 128), i32),
            vmem((2, 2 * BANDS, 64), bf16),
            vmem((2, 2, RING, 64, 128), bf16),
            vmem((2, RING, 2, STAT, BLOCK), bf16),
            vmem((STAGES, 32, STAT, WIDTH), bf16),
            vmem((STAGES, 2, RING, CORES, STAT, WIDTH), bf16),
            vmem((CORES, RING, 2, 2, 64, 128), bf16),
            vmem((CORES, RING, 2, 2, STAT, BLOCK), bf16),
            vmem((STAGES, 2, RING, 64, COLS), f32),
            vmem((STAGES, RING, 2, 64, COLS), bf16),
            vmem((STAGES, RING, CORES, 2, STAT, HALF), f32),
            vmem((STAGES, RING, CORES, 2, STAT, HALF), bf16),
            vmem((STAGES, 2, 2, STAT, HALF), bf16),
            vmem((STAGES, 2, 2, STAT, HALF), bf16),
            vmem((CORES, STAGES, 2, 2, STAT, HALF), bf16),
            vmem((STAGES, 2, STAT, HALF), f32),
            dma((3,)), dma((STAGES,)), dma((STAGES,)), dma((STAGES,)), dma((3,)), dma((STAGES,)),
            dma((STAGES,)), dma((STAGES,)), dma((STAGES,)), dma((STAGES, CORES, 3)), dma((STAGES, CORES, 4, 3)),
            dma((STAGES, CORES, 3)), dma((4,)), dma((STAGES, 2, 2)), dma((CORES, STAGES, 2)), dma((STAGES,)),
        ],
        compiler_params=pltpu.CompilerParams(
            collective_id=0, has_side_effects=True, vmem_limit_bytes=48 * 1024 * 1024
        ),
    )(spectra, bins, table)


def per_device(records, ref_bin, ref_table):
    spectra = records.reshape(STAT, 2, 16, 128).transpose(0, 2, 1, 3).reshape(STAT * 32, 128)
    args = (spectra, ref_bin.reshape(1024, 128), ref_table.T)
    out = exchange(*(pltpu.with_memory_space_constraint(arg, pltpu.HBM) for arg in args))
    return out.reshape(STAT, 16, 2, 128).transpose(0, 2, 1, 3).reshape(STAT, 2, 2048)


def solution(mesh):
    in_specs = (P(("grp", "sub"), None, None), P("grp", None, "sub", None), P())
    out_specs = P(("grp", "sub"), None, None)
    return jax.shard_map(
        per_device, mesh=mesh, in_specs=in_specs, out_specs=out_specs, check_vma=False
    )
```
